512 devices in a mesh: section: 8 (over y, x_lo), tile: 64 (over z, x_hi, core).
Axes of the slice: x: 4 (x_hi: 2, x_lo: 2; x = x_hi * 2 + x_lo), y: 4, z: 16, core: 2. Of those that a mesh axis runs over, the one named last changes fastest.
Arguments:
- block_inputs: bfloat16 [8, 24576, 1536], P('section', 'tile'), may hold values from -6 to 6
- stale_kv: bfloat16 [8, 24576, 3072], P('section', 'tile'), may hold values from -6 to 6
- projection: bfloat16 [8, 3, 1536, 1536], P('section', None, None, 'tile'), may hold values from -0.15625 to 0.15625
- modulation: float32 [8, 3, 1536], P('section'), may hold values from -3 to 3
- pattern: int32 [128, 4], P('tile'), may hold values from 0 to 1, as said below
- order: int32 [2], replicated, may hold values from 0 to 1, each once
Outputs:
- block_outputs: bfloat16 [8, 24576, 1536], P('section', 'tile')
The draws below stay inside these ranges and needn't reach their ends.
Inputs may be any that keep to these rules, and one draw needn't show every extreme that they name: `pattern`: row i has a 1 at entry 1 + (i mod 2), its own tile, and at entries 0 and 3. `order`: each of the 2 patch groups appears once.
All inputs are finite; a program needn't handle non-finite values.
Results may differ from the reference program's by a relative error of at most 0.0039.
Values may be sent and summed in bfloat16 or wider, within the bound.
A program may use at most 128 MiB of HBM per device.

```python
import math
import jax
import jax.numpy as jnp
import numpy as np
from jax import lax

HEADS = 12
FEAT = 1536
TILE_TOK = 192
RIM = 48
GROUPS = 2
TPG = 1
TPD = 2
TOK_DEV = 384
TILES = 128
TOKENS = 24576
SECTIONS = 8
N_SECTION = 8
N_TILE = 64


def draw_pattern(key, part):
    key = jax.random.fold_in(key, 7)
    coin_flips = jax.random.randint(key, (TILES, TPD + 2), 0, 5)
    linked = (coin_flips < 3).astype(jnp.int32)
    own_slot = jnp.arange(TILES, dtype=jnp.int32)[:, None] % TPD + 1
    slot_ids = jnp.arange(TPD + 2, dtype=jnp.int32)[None, :]
    forced = (slot_ids == own_slot) | (slot_ids == 0) | (slot_ids == TPD + 1)
    return jnp.where(forced, 1, linked).astype(jnp.int32)


def steps_of(own_key, extent, cuts, least, largest):
    loudness, own = 1.0, jax.random.fold_in(own_key, 6)
    for dim, parts in cuts:
        steps = jnp.exp(jax.random.uniform(jax.random.fold_in(own, dim), (parts,), jnp.float32, least / len(cuts), largest / len(cuts)))
        loudness = loudness * jnp.repeat(steps, extent[dim] // parts).reshape([-1 if axis == dim else 1 for axis in range(len(extent))])
    return loudness


def normal_values(stream_key, dims, scale, bound, cuts=(), held_as=jnp.bfloat16):
    loudness = steps_of(stream_key, dims, cuts, -0.22, 0.18) if cuts else 1.0
    values = jax.random.normal(stream_key, dims, jnp.float32) * scale * loudness
    return jnp.minimum(jnp.maximum(values, -bound), bound).astype(held_as)


def setup_inputs(seed: int = 0) -> dict:
    key_of = jax.random.split(jax.random.key(seed), 7)
    block_inputs = normal_values(key_of[0], (SECTIONS, TOKENS, FEAT), 1.0, 6.0, ((0, 8), (1, 64)))
    stale_kv = normal_values(key_of[1], (SECTIONS, TOKENS, 2 * FEAT), 1.0, 6.0, ((0, 8), (1, 64)))
    projection = normal_values(key_of[2], (SECTIONS, 3, FEAT, FEAT), FEAT ** -0.5, 0.15625, ((0, 8), (3, 64)))
    modulation = normal_values(key_of[3], (SECTIONS, 3, FEAT), 0.5, 3.0, ((0, 8),), jnp.float32)
    pattern = draw_pattern(jax.random.fold_in(key_of[6], 71), 0)
    order = jax.random.permutation(key_of[5], GROUPS).astype(jnp.int32)
    return dict(block_inputs=block_inputs, stale_kv=stale_kv, projection=projection, modulation=modulation, pattern=pattern, order=order)


epsilon = 1e-06

def modulate(stream, modulation_row):
    values = stream.astype(jnp.float32)
    normed = values * lax.rsqrt(lax.optimization_barrier(jnp.mean(values * values, axis=-1, keepdims=True)) + epsilon)
    return ((1.0 + modulation_row[1]) * normed + modulation_row[0]).astype(jnp.bfloat16)

def head_norm(values, head_count):
    shaped = values.reshape(values.shape[0], head_count, -1)
    shaped = shaped * lax.rsqrt(lax.optimization_barrier(jnp.mean(shaped * shaped, axis=-1, keepdims=True)) + epsilon)
    return shaped.reshape(values.shape).astype(jnp.bfloat16)

def keys_values(hidden, key_weight, value_weight, head_count):
    key_rows = jnp.dot(hidden, key_weight, preferred_element_type=jnp.float32)
    value_rows = jnp.dot(hidden, value_weight, preferred_element_type=jnp.float32)
    return jnp.concatenate([head_norm(key_rows, head_count), value_rows.astype(jnp.bfloat16)], axis=-1)

def attend_batch(queries, window, allowed, head_count):
    batch_size, row_count, feat_width = queries.shape
    head_width = feat_width // head_count
    query_heads = queries.astype(jnp.float32).reshape(batch_size, row_count, head_count, head_width)
    key_heads = window[..., :feat_width].astype(jnp.float32).reshape(batch_size, -1, head_count, head_width)
    value_heads = window[..., feat_width:].astype(jnp.float32).reshape(batch_size, -1, head_count, head_width)
    scores = jnp.einsum('bqhd,bkhd->bhqk', query_heads, key_heads) * (1.0 / math.sqrt(head_width))
    unnormed = jnp.exp(scores) * allowed[:, None].astype(jnp.float32)
    weights_low = (unnormed / lax.optimization_barrier(jnp.sum(unnormed, axis=-1, keepdims=True))).astype(jnp.bfloat16)
    attended = jnp.einsum('bhqk,bkhd->bqhd', weights_low.astype(jnp.float32), value_heads)
    return attended.reshape(batch_size, row_count, feat_width)

def windows(key_value):
    shaped = key_value.reshape(N_TILE, TOK_DEV, -1)
    padded = jnp.pad(shaped, ((1, 1), (0, 0), (0, 0)))
    return jnp.concatenate([padded[:-2, -RIM:], shaped, padded[2:, :RIM]], axis=1)

def reference(block_inputs, stale_kv, projection, modulation, pattern, order):
    group_ids = jnp.arange(GROUPS, dtype=jnp.int32)
    position = lax.optimization_barrier(jnp.sum(group_ids[:, None] * (order[:, None] == group_ids[None, :]).astype(jnp.int32), axis=0)).astype(jnp.int32)
    slot_groups = np.concatenate([np.array([(TPD - 1) % GROUPS]), np.arange(TPD) % GROUPS, np.array([0])]).astype(np.int32)
    token_groups = (np.arange(TOKENS) // TILE_TOK % TPD % GROUPS).astype(np.int32)
    rim_slot = np.zeros(TPD + 2, dtype=bool)
    rim_slot[0] = True
    rim_slot[TPD + 1] = True
    slot_tokens = np.array([RIM] + [TILE_TOK] * TPD + [RIM], dtype=np.int32)
    window_len = TOK_DEV + 2 * RIM
    slot_valid = np.ones((N_TILE, TPD + 2), dtype=bool)
    slot_valid[0, 0] = False
    slot_valid[N_TILE - 1, TPD + 1] = False
    tile_mask = (pattern.reshape(N_TILE, TPD, TPD + 2) > 0) & jnp.asarray(slot_valid)[:, None, :]
    tile_mask = tile_mask.reshape(N_TILE, TPG, GROUPS, TPD + 2)
    outputs = []
    for section_id in range(N_SECTION):
        turn = ((position + section_id) % GROUPS).astype(jnp.int32)
        if section_id == 0:
            stream = block_inputs[0]
        else:
            stale_rows = turn[jnp.asarray(token_groups)] == 0
            stream = jnp.where(stale_rows[:, None], block_inputs[section_id], outputs[-1])
        weights = projection[section_id]
        modulation_row = modulation[section_id]
        hidden = modulate(stream, modulation_row)
        queries = head_norm(jnp.dot(hidden, weights[0], preferred_element_type=jnp.float32), HEADS)
        fresh_window = windows(keys_values(hidden, weights[1], weights[2], HEADS))
        stale_window = windows(stale_kv[section_id])
        query_tiles = queries.reshape(N_TILE, TPG, GROUPS, TILE_TOK, FEAT)
        blocks = jnp.zeros((N_TILE, TPG, GROUPS, TILE_TOK, FEAT), jnp.float32)
        slot_turn = turn[jnp.asarray(slot_groups)]
        for group_id in range(GROUPS):
            fresh_slots = jnp.where(jnp.asarray(rim_slot), slot_turn < turn[group_id], slot_turn <= turn[group_id])
            fresh_tokens = jnp.repeat(fresh_slots, slot_tokens, total_repeat_length=window_len)
            window = jnp.where(fresh_tokens[None, :, None], fresh_window, stale_window)
            allowed = tile_mask[:, :, group_id]
            allowed = jnp.repeat(allowed, TILE_TOK, axis=1)
            allowed = jnp.repeat(allowed, slot_tokens, axis=2, total_repeat_length=window_len)
            chosen = query_tiles[:, :, group_id].reshape(N_TILE, TPG * TILE_TOK, FEAT)
            result = attend_batch(chosen, window, allowed, HEADS)
            blocks = blocks.at[:, :, group_id].set(result.reshape(N_TILE, TPG, TILE_TOK, FEAT))
        attended = blocks.reshape(TOKENS, FEAT)
        new_stream = (stream.astype(jnp.float32) + modulation_row[2] * attended).astype(jnp.bfloat16)
        outputs.append(new_stream)
    return jnp.stack(outputs)
```

```python
import math

import jax
import jax.numpy as jnp
from jax import lax
from jax.experimental import pallas as pl
from jax.experimental.pallas import tpu as pltpu
from jax.sharding import PartitionSpec as P

HEADS = 12
FEAT = 1536
TILE = 192
RIM = 48
PLANES = 16
SECTIONS = 8
TILES = 64
COLS = 24
GROUPS = 4
WIDE = FEAT // GROUPS
HEAD = FEAT // HEADS
WINDOW = 2 * TILE + 2 * RIM
EPS = 1e-06
MESH = pl.DeviceIdType.MESH
NT = (((1,), (1,)), ((), ()))


def kernel(
    x_hbm, stale_hbm, proj_hbm, mod_ref, pattern_ref, order_ref, out_ref,
    w, dense, xb, st, hidden, q, kv, o, rs, sl, su, fl, fu,
    loc_sem, zs, zr, xs, xr, d1s, d1r, d2s, d2r, rim_s, rim_r, fr_s, fr_r, str_s, str_r,
):
    section = lax.axis_index("section")
    tile = lax.axis_index("tile")
    z = tile // 4
    xh = (tile // 2) % 2
    c = tile % 2
    u = xh * 2 + c
    up = (1 - xh) * 2 + c

    def plane(d):
        return (z + d + PLANES) % PLANES

    def at_tile(t):
        return (section, t)

    z_dev = (
        at_tile(((z + 1) % PLANES) * 4 + u),
        at_tile(((z + PLANES - 1) % PLANES) * 4 + u),
    )
    x_dev = at_tile(z * 4 + up)
    sib = at_tile(z * 4 + xh * 2 + (1 - c))
    tile_hi = at_tile((tile + 1) % TILES)
    tile_lo = at_tile((tile + TILES - 1) % TILES)
    sec_hi = ((section + 1) % SECTIONS, tile)
    sec_lo = ((section + SECTIONS - 1) % SECTIONS, tile)

    own_w = pltpu.make_async_copy(proj_hbm, w.at[z, u], loc_sem.at[0])
    own_w.start()
    x_loads = [
        pltpu.make_async_copy(x_hbm.at[:, pl.ds(g * WIDE, WIDE)], xb.at[g], loc_sem.at[1 + g])
        for g in range(GROUPS)
    ]
    st_loads = [
        pltpu.make_async_copy(
            stale_hbm.at[:, pl.ds((k * GROUPS + g) * WIDE, WIDE)], st.at[g, k],
            loc_sem.at[5 + 2 * g + k],
        )
        for g in range(GROUPS)
        for k in range(2)
    ]
    for cp in x_loads + st_loads:
        cp.start()

    bar = pltpu.get_barrier_semaphore()
    peers = (z_dev[0], z_dev[1], x_dev, sib, tile_hi, tile_lo, sec_hi, sec_lo)
    for dev in peers:
        pl.semaphore_signal(bar, inc=1, device_id=dev, device_id_type=MESH)
    pl.semaphore_wait(bar, len(peers))

    def remote(src, dst, s, r, dev):
        return pltpu.make_async_remote_copy(
            src_ref=src, dst_ref=dst, send_sem=s, recv_sem=r, device_id=dev, device_id_type=MESH
        )

    def z_copy(part, way, p):
        if part == 0:
            ref = w.at[p, u, pl.ds(0, 2)]
        elif part == 1:
            ref = w.at[p, u, 2]
        else:
            ref = w.at[p, up, 2]
        return remote(ref, ref, zs.at[part, way, p], zr.at[part, p], z_dev[way])

    def z_wait(part, p):
        z_copy(part, 0, p).wait_recv()

    def x_copy(p):
        ref = w.at[p, u, pl.ds(0, 2)]
        return remote(ref, ref, xs.at[p], xr.at[p], x_dev)

    def x_own():
        ref = w.at[z, u]
        return remote(ref, ref, xs.at[z], xr.at[z], x_dev)

    def d1_copy(p):
        ref = w.at[p, u]
        return remote(ref, ref, d1s.at[p], d1r.at[p], sib)

    def d2_copy(p):
        ref = w.at[p, up]
        return remote(ref, ref, d2s.at[p], d2r.at[p], sib)

    own_w.wait()
    x_own().start()
    for way in range(2):
        z_copy(0, way, z).start()
    for way in range(2):
        z_copy(1, way, z).start()
    d1_copy(z).start()

    for cp in st_loads:
        cp.wait()
    rim_up = remote(st.at[:, :, pl.ds(0, RIM), :], su, rim_s.at[0], rim_r.at[0], tile_lo)
    rim_down = remote(
        st.at[:, :, pl.ds(2 * TILE - RIM, RIM), :], sl, rim_s.at[1], rim_r.at[1], tile_hi
    )

    parity = section % 2
    first = order_ref[0:1, 0:1]
    second = order_ref[0:1, 1:2]
    j0 = jnp.where(parity == 0, first, second)
    has_lo = jnp.where(tile > 0, 1, 0)
    has_hi = jnp.where(tile < TILES - 1, 1, 0)

    def pick(flag, yes, no):
        on = jnp.broadcast_to(flag, yes.shape) > 0
        return jnp.where(on, yes.astype(jnp.float32), no.astype(jnp.float32))

    def mask_of(j):
        def mark(slot):
            one, two = pattern_ref[0:1, slot : slot + 1], pattern_ref[1:2, slot : slot + 1]
            return one + j * (two - one)

        one, two = mark(1), mark(2)
        spans = (
            (one + j0 * (two - one), TILE),
            (two + j0 * (one - two), TILE),
            (mark(0) * has_lo, RIM),
            (mark(3) * has_hi, RIM),
        )
        lane = lax.broadcasted_iota(jnp.int32, (1, WINDOW), 1)
        marks = jnp.zeros((1, WINDOW), jnp.int32)
        start = 0
        for value, width in spans:
            inside = (lane >= start) & (lane < start + width)
            marks = jnp.where(inside, jnp.broadcast_to(value, marks.shape), marks)
            start += width
        return jnp.where(marks > 0, 1.0, 0.0)

    def tile_rows(ref, g, j):
        return pick(j, ref[g, TILE : 2 * TILE, :], ref[g, 0:TILE, :])

    def stale_other(g, n):
        one, two = st[g, n, 0:TILE, :], st[g, n, TILE : 2 * TILE, :]
        return pick(j0, one, two).astype(jnp.bfloat16)

    def modulate(parts):
        total = jnp.zeros((TILE, 1), jnp.float32)
        for part in parts:
            values = part().astype(jnp.float32)
            total = total + jnp.sum(values * values, axis=1, keepdims=True)
        inv = lax.rsqrt(total * (1.0 / FEAT) + EPS)
        for g, part in enumerate(parts):
            cols = pl.ds(g * WIDE, WIDE)
            normed = part().astype(jnp.float32) * inv
            hidden[:, cols] = (
                (1.0 + mod_ref[1:2, cols]) * normed + mod_ref[0:1, cols]
            ).astype(jnp.bfloat16)

    def head_norm(rows):
        parts = []
        for h in range(WIDE // HEAD):
            one = rows[:, h * HEAD : (h + 1) * HEAD]
            mean = jnp.mean(one * one, axis=1, keepdims=True)
            parts.append(one * lax.rsqrt(mean + EPS))
        return jnp.concatenate(parts, axis=1).astype(jnp.bfloat16)

    def project(turn, g):
        rows = hidden[...]
        for m in range(3):
            weight = dense[g, m].reshape(WIDE, FEAT)
            res = lax.dot_general(rows, weight, NT, preferred_element_type=jnp.float32)
            if m == 0:
                q[g] = head_norm(res)
            elif m == 1:
                kv[turn, g, 0] = head_norm(res)
            else:
                kv[turn, g, 1] = res.astype(jnp.bfloat16)

    def attend(g, mask, other, low, high, stream, turn):
        def window(k):
            return jnp.concatenate([kv[0, g, k], other(k), low(k), high(k)], axis=0)

        keys = window(0)
        values = window(1)
        queries = q[g]
        outs = []
        for h in range(WIDE // HEAD):
            cols = slice(h * HEAD, (h + 1) * HEAD)
            scores = lax.dot_general(
                queries[:, cols], keys[:, cols], NT, preferred_element_type=jnp.float32
            ) * (1.0 / math.sqrt(HEAD))
            unnormed = jnp.exp(scores) * mask
            total = jnp.sum(unnormed, axis=1, keepdims=True)
            weights = (unnormed / total).astype(jnp.bfloat16)
            outs.append(jnp.dot(weights, values[:, cols], preferred_element_type=jnp.float32))
        attended = jnp.concatenate(outs, axis=1)
        gate = mod_ref[2:3, pl.ds(pl.multiple_of(g * WIDE, WIDE), WIDE)]
        o[turn, g] = (stream.astype(jnp.float32) + gate * attended).astype(jnp.bfloat16)

    def lay_out(p):
        d1_copy(p).wait_recv()
        d2_copy(p).wait_recv()
        for m in range(3):
            parts = [w[p, v, m].astype(jnp.float32) for v in range(4)]
            dense[p // 4, m, p % 4] = jnp.concatenate(parts, axis=0).astype(jnp.bfloat16)

    def rim_fresh(g):
        up_copy = remote(
            kv.at[0, g, :, pl.ds(0, RIM), :], fu.at[g], fr_s.at[0, g], fr_r.at[0, g], tile_lo
        )
        down_copy = remote(
            kv.at[0, g, :, pl.ds(TILE - RIM, RIM), :], fl.at[g], fr_s.at[1, g], fr_r.at[1, g],
            tile_hi,
        )
        return up_copy, down_copy

    def stream_copy(g):
        return remote(o.at[0, g], rs.at[g], str_s.at[g], str_r.at[g], sec_hi)

    near = jnp.where(z % 4 < 2, GROUPS - 1, 1)

    def group_at(k):
        base = z // 4
        step = jnp.where(k == 0, 0, jnp.where(k == 1, near, jnp.where(k == 2, GROUPS - near, 2)))
        return (base + step) % GROUPS

    def first_turn(k):
        g = group_at(k)
        project(0, g)
        for cp in rim_fresh(g):
            cp.start()
        attend(
            g, mask_of(j0), lambda n: stale_other(g, n), lambda n: sl[g, n],
            lambda n: su[g, n], tile_rows(xb, g, j0), 0,
        )
        stream_copy(g).start()

    x_own().wait_recv()
    for way in range(2):
        z_copy(2, way, z).start()
    d2_copy(z).start()
    rim_up.start()
    rim_down.start()

    for cp in x_loads:
        cp.wait()
    modulate([lambda g=g: tile_rows(xb, g, j0) for g in range(GROUPS)])
    rim_up.wait_recv()
    rim_down.wait_recv()

    def ring_step(s, carry):
        before = plane(-s)
        after = plane(s)

        @pl.when(s <= 8)
        def _():
            z_wait(0, before)

            @pl.when(s <= 7)
            def _():
                z_copy(0, 0, before).start()

            x_copy(before).start()

        @pl.when(s <= 7)
        def _():
            z_wait(0, after)

            @pl.when(s <= 6)
            def _():
                z_copy(0, 1, after).start()

            x_copy(after).start()

        @pl.when(s >= 2)
        def _():
            p = plane(1 - s)
            x_copy(p).wait_recv()
            d2_copy(p).start()

        @pl.when((s >= 2) & (s <= 8))
        def _():
            p = plane(s - 1)
            x_copy(p).wait_recv()
            d2_copy(p).start()

        @pl.when(s <= 7)
        def _():
            for part in (1, 2):
                z_wait(part, before)

                @pl.when(s <= 6)
                def _():
                    z_copy(part, 0, before).start()

            d1_copy(before).start()

        @pl.when(s <= 8)
        def _():
            for part in (1, 2):
                z_wait(part, after)

                @pl.when(s <= 7)
                def _():
                    z_copy(part, 1, after).start()

            d1_copy(after).start()

        lay_out(plane(1 - s))

        @pl.when((s >= 2) & (s <= 8))
        def _():
            lay_out(plane(s - 1))

        @pl.when((s == 4) | (s == 6) | (s >= 8))
        def _():
            first_turn(jnp.where(s == 9, 3, (s - 4) // 2))

        return carry

    lax.fori_loop(1, 10, ring_step, 0)

    for g in range(GROUPS):
        stream_copy(g).wait_recv()
    is_first = section == 0

    def second_stream(g):
        return jnp.where(is_first, tile_rows(xb, g, 1 - j0), rs[g].astype(jnp.float32))

    modulate([lambda g=g: second_stream(g) for g in range(GROUPS)])
    for g in range(GROUPS):
        for cp in rim_fresh(g):
            cp.wait_recv()

    def second_turn(g, carry):
        project(1, g)
        attend(
            g, mask_of(1 - j0), lambda n: kv[1, g, n],
            lambda n: pick(j0, fl[g, n], sl[g, n]).astype(jnp.bfloat16),
            lambda n: pick(j0, su[g, n], fu[g, n]).astype(jnp.bfloat16),
            second_stream(g), 1,
        )
        return carry

    lax.fori_loop(0, GROUPS, second_turn, 0)
    for g in range(GROUPS):
        cols = pl.ds(g * WIDE, WIDE)
        out_ref[pl.ds(0, TILE), cols] = pick(j0, o[1, g], o[0, g]).astype(jnp.bfloat16)
        out_ref[pl.ds(TILE, TILE), cols] = pick(j0, o[0, g], o[1, g]).astype(jnp.bfloat16)

    x_own().wait_send()
    rim_up.wait_send()
    rim_down.wait_send()
    for part in range(3):
        for way in range(2):
            z_copy(part, way, z).wait_send()
    d1_copy(z).wait_send()
    d2_copy(z).wait_send()
    for g in range(GROUPS):
        for cp in rim_fresh(g):
            cp.wait_send()
        stream_copy(g).wait_send()

    def drain(s, carry):
        before = plane(-s)
        after = plane(s)
        z_copy(0, 0, before).wait_send()
        x_copy(before).wait_send()
        d1_copy(before).wait_send()
        d2_copy(before).wait_send()
        for part in (1, 2):
            z_copy(part, 1, after).wait_send()

        @pl.when(s <= 6)
        def _():
            z_copy(0, 1, after).wait_send()
            for part in (1, 2):
                z_copy(part, 0, before).wait_send()

        x_copy(after).wait_send()
        d1_copy(after).wait_send()
        d2_copy(after).wait_send()
        return carry

    lax.fori_loop(1, 8, drain, 0)
    far = plane(8)
    x_copy(far).wait_send()
    d1_copy(far).wait_send()
    d2_copy(far).wait_send()


def shards(block_inputs, stale_kv, projection, modulation, pattern, order):
    dma = pltpu.SemaphoreType.DMA
    vmem = pltpu.VMEM
    bf16 = jnp.bfloat16
    out = pl.pallas_call(
        kernel,
        out_shape=jax.ShapeDtypeStruct((2 * TILE, FEAT), bf16),
        in_specs=[pl.BlockSpec(memory_space=pl.ANY)] * 3
        + [pl.BlockSpec(memory_space=pltpu.VMEM)] * 3,
        out_specs=pl.BlockSpec(memory_space=pltpu.VMEM),
        scratch_shapes=[
            vmem((PLANES, 4, 3, COLS, FEAT), bf16),
            vmem((GROUPS, 3, 4, 4 * COLS, FEAT), bf16),
            vmem((GROUPS, 2 * TILE, WIDE), bf16),
            vmem((GROUPS, 2, 2 * TILE, WIDE), bf16),
            vmem((TILE, FEAT), bf16),
            vmem((GROUPS, TILE, WIDE), bf16),
            vmem((2, GROUPS, 2, TILE, WIDE), bf16),
            vmem((2, GROUPS, TILE, WIDE), bf16),
            vmem((GROUPS, TILE, WIDE), bf16),
            vmem((GROUPS, 2, RIM, WIDE), bf16),
            vmem((GROUPS, 2, RIM, WIDE), bf16),
            vmem((GROUPS, 2, RIM, WIDE), bf16),
            vmem((GROUPS, 2, RIM, WIDE), bf16),
            dma((13,)),
            dma((3, 2, PLANES)),
            dma((3, PLANES)),
            dma((PLANES,)),
            dma((PLANES,)),
            dma((PLANES,)),
            dma((PLANES,)),
            dma((PLANES,)),
            dma((PLANES,)),
            dma((2,)),
            dma((2,)),
            dma((2, GROUPS)),
            dma((2, GROUPS)),
            dma((GROUPS,)),
            dma((GROUPS,)),
        ],
        compiler_params=pltpu.CompilerParams(
            collective_id=0, has_side_effects=True, vmem_limit_bytes=58 * 2**20
        ),
        name="blocks",
    )(
        block_inputs[0],
        stale_kv[0],
        jnp.swapaxes(projection[0], 1, 2),
        modulation[0],
        pattern,
        order.reshape(1, 2),
    )
    return out[None]


def solution(mesh):
    placed = (
        P("section", "tile", None),
        P("section", "tile", None),
        P("section", None, None, "tile"),
        P("section", None, None),
        P("tile", None),
        P(),
    )
    return jax.shard_map(
        shards, mesh=mesh, in_specs=placed, out_specs=P("section", "tile", None), check_vma=False
    )
```

```python
import math

import jax
import jax.numpy as jnp
from jax import lax
from jax.experimental import pallas as pl
from jax.experimental.pallas import tpu as pltpu
from jax.sharding import PartitionSpec as P

HEADS = 12
FEAT = 1536
TILE = 192
RIM = 48
PLANES = 16
SECTIONS = 8
TILES = 64
COLS = 24
GROUPS = 4
WIDE = FEAT // GROUPS
HEAD = FEAT // HEADS
WINDOW = 2 * TILE + 2 * RIM
DUP = 768
EPS = 1e-06
MESH = pl.DeviceIdType.MESH
NT = (((1,), (1,)), ((), ()))
SCALE = math.log2(math.e) / math.sqrt(HEAD)


def kernel(
    x_hbm, stale_hbm, proj_hbm, mod_hbm, pattern_ref, order_ref, out_ref,
    w, dense, xb, st, hidden, q, kv, o, rs, sl, su, xl, xu, fr, marks, mod_ref,
    loc_sem, zs, zr, xs, xr, d1s, d1r, d2s, d2r, rim_s, rim_r, str_s, str_r, out_sem,
):
    section = lax.axis_index("section")
    tile = lax.axis_index("tile")
    z = tile // 4
    xh = (tile // 2) % 2
    c = tile % 2
    u = xh * 2 + c
    up = (1 - xh) * 2 + c

    def plane(d):
        return (z + d + PLANES) % PLANES

    def at_tile(t):
        return (section, t)

    z_dev = (
        at_tile(((z + 1) % PLANES) * 4 + u),
        at_tile(((z + PLANES - 1) % PLANES) * 4 + u),
    )
    x_dev = at_tile(z * 4 + up)
    sib = at_tile(z * 4 + xh * 2 + (1 - c))
    tile_hi = at_tile((tile + 1) % TILES)
    tile_lo = at_tile((tile + TILES - 1) % TILES)
    sec_hi = ((section + 1) % SECTIONS, tile)
    sec_lo = ((section + SECTIONS - 1) % SECTIONS, tile)

    own_w = pltpu.make_async_copy(proj_hbm, w.at[z, u], loc_sem.at[0])
    own_w.start()
    x_loads = [
        pltpu.make_async_copy(x_hbm.at[:, pl.ds(g * WIDE, WIDE)], xb.at[g], loc_sem.at[1 + g])
        for g in range(GROUPS)
    ]
    st_loads = [
        pltpu.make_async_copy(
            stale_hbm.at[:, pl.ds((k * GROUPS + g) * WIDE, WIDE)], st.at[g, k],
            loc_sem.at[5 + 2 * g + k],
        )
        for g in range(GROUPS)
        for k in range(2)
    ]
    mod_loads = [
        pltpu.make_async_copy(mod_hbm.at[m], mod_ref.at[pl.ds(m, 1)], loc_sem.at[13 + m])
        for m in range(3)
    ]
    for cp in x_loads + st_loads + mod_loads:
        cp.start()

    bar = pltpu.get_barrier_semaphore()
    peers = (z_dev[0], z_dev[1], x_dev, sib, tile_hi, tile_lo, sec_hi, sec_lo)
    for dev in peers:
        pl.semaphore_signal(bar, inc=1, device_id=dev, device_id_type=MESH)
    pl.semaphore_wait(bar, len(peers))

    def remote(src, dst, s, r, dev):
        return pltpu.make_async_remote_copy(
            src_ref=src, dst_ref=dst, send_sem=s, recv_sem=r, device_id=dev, device_id_type=MESH
        )

    def z_copy(part, way, p):
        if part == 0:
            ref = w.at[p, u, pl.ds(0, 2)]
        elif part == 1:
            ref = w.at[p, u, 2]
        elif part == 2:
            ref = w.at[p, up, 2]
        else:
            ref = w.at[p, up, 1, :, pl.ds(0, DUP)]
        return remote(ref, ref, zs.at[part, way, p], zr.at[part, p], z_dev[way])

    def z_wait(part, p):
        z_copy(part, 0, p).wait_recv()

    def x_copies(p):
        refs = (w.at[p, u, 0], w.at[p, u, 1, :, pl.ds(DUP, FEAT - DUP)])
        return [
            remote(ref, ref, xs.at[i, p], xr.at[i, p], x_dev) for i, ref in enumerate(refs)
        ]

    def x_own():
        refs = (w.at[z, u, 0], w.at[z, u, pl.ds(1, 2)])
        return [
            remote(ref, ref, xs.at[i, z], xr.at[i, z], x_dev) for i, ref in enumerate(refs)
        ]

    def x_start(p):
        for cp in x_copies(p):
            cp.start()

    def x_wait(p):
        for cp in x_copies(p):
            cp.wait_recv()

    def x_drain(p):
        for cp in x_copies(p):
            cp.wait_send()

    def d1_copy(p):
        ref = w.at[p, u]
        return remote(ref, ref, d1s.at[p], d1r.at[p], sib)

    def d2_copy(p):
        ref = w.at[p, up]
        return remote(ref, ref, d2s.at[p], d2r.at[p], sib)

    own_w.wait()
    x_own()[1].start()
    x_own()[0].start()
    for part in (0, 1):
        for way in range(2):
            z_copy(part, way, z).start()
    d1_copy(z).start()

    head_rows = pl.ds(0, RIM)
    tail_rows = pl.ds(2 * TILE - RIM, RIM)
    rims = [
        remote(st.at[:, :, head_rows, :], su, rim_s.at[0], rim_r.at[0], tile_lo),
        remote(st.at[:, :, tail_rows, :], sl, rim_s.at[1], rim_r.at[1], tile_hi),
        remote(xb.at[:, head_rows, :], xu, rim_s.at[2], rim_r.at[2], tile_lo),
        remote(xb.at[:, tail_rows, :], xl, rim_s.at[3], rim_r.at[3], tile_hi),
    ]

    parity = section % 2
    first = order_ref[0:1, 0:1]
    second = order_ref[0:1, 1:2]
    j0 = jnp.where(parity == 0, first, second)
    has_lo = jnp.where(tile > 0, 1, 0)
    has_hi = jnp.where(tile < TILES - 1, 1, 0)

    def pick(flag, yes, no):
        on = jnp.broadcast_to(flag, yes.shape) > 0
        return jnp.where(on, yes.astype(jnp.float32), no.astype(jnp.float32))

    def set_marks(turn, j):
        def mark(slot):
            one, two = pattern_ref[0:1, slot : slot + 1], pattern_ref[1:2, slot : slot + 1]
            return one + j * (two - one)

        one, two = mark(1), mark(2)
        spans = (
            (one + j0 * (two - one), TILE),
            (two + j0 * (one - two), TILE),
            (mark(0) * has_lo, RIM),
            (mark(3) * has_hi, RIM),
        )
        start = 0
        for value, width in spans:
            on = jnp.broadcast_to(value, (width, HEAD)) > 0
            marks[turn, pl.ds(start, width), :] = jnp.where(on, 1.0, 0.0).astype(jnp.bfloat16)
            start += width

    def tile_rows(ref, g, j):
        return pick(j, ref[g, TILE : 2 * TILE, :], ref[g, 0:TILE, :])

    def stale_other(g, n):
        one, two = st[g, n, 0:TILE, :], st[g, n, TILE : 2 * TILE, :]
        return pick(j0, one, two).astype(jnp.bfloat16)

    def modulate(parts, start, count):
        total = jnp.zeros((count, 1), jnp.float32)
        for part in parts:
            values = part()
            total = total + jnp.sum(values * values, axis=1, keepdims=True)
        inv = lax.rsqrt(total * (1.0 / FEAT) + EPS)
        for g, part in enumerate(parts):
            cols = pl.ds(g * WIDE, WIDE)
            normed = part() * inv
            hidden[pl.ds(start, count), cols] = (
                (1.0 + mod_ref[1:2, cols]) * normed + mod_ref[0:1, cols]
            ).astype(jnp.bfloat16)

    def head_norm(rows, factor):
        parts = []
        for h in range(WIDE // HEAD):
            one = rows[:, h * HEAD : (h + 1) * HEAD]
            mean = jnp.mean(one * one, axis=1, keepdims=True)
            parts.append(one * (lax.rsqrt(mean + EPS) * factor))
        return jnp.concatenate(parts, axis=1).astype(jnp.bfloat16)

    def project(turn, g):
        count = TILE + RIM if turn == 0 else TILE
        rows = hidden[pl.ds(0, count), :]
        for m in range(3):
            weight = dense[g, m].reshape(WIDE, FEAT)
            res = lax.dot_general(
                rows if m else rows[0:TILE], weight, NT, preferred_element_type=jnp.float32
            )
            low = head_norm(res, 1.0 if m else SCALE) if m < 2 else res.astype(jnp.bfloat16)
            if m == 0:
                q[g] = low
                continue
            kv[turn, g, m - 1] = low[0:TILE]
            if turn == 0:
                fr[g, m - 1] = low[TILE:count]

    def attend(g, turn, other, low, high, stream, ready):
        def window(k):
            return jnp.concatenate([kv[0, g, k], other(k), low(k), high(k)], axis=0)

        keys = window(0)
        values = window(1)
        queries = q[g]
        mark = marks[turn]
        gate = mod_ref[2:3, pl.ds(pl.multiple_of(g * WIDE, WIDE), WIDE)]
        for h in range(WIDE // HEAD):
            cols = slice(h * HEAD, (h + 1) * HEAD)
            scores = lax.dot_general(
                queries[:, cols], keys[:, cols], NT, preferred_element_type=jnp.float32
            )
            unnormed = jnp.exp2(scores).astype(jnp.bfloat16)
            marked = jnp.concatenate([values[:, cols] * mark, mark], axis=1)
            both = jnp.dot(unnormed, marked, preferred_element_type=jnp.float32)
            attended = both[:, :HEAD] / both[:, HEAD:]
            o[turn, g, :, cols] = (stream[:, cols] + gate[:, cols] * attended).astype(jnp.bfloat16)
            ready(g, h)
        out_copy(turn, g).start()

    def out_copy(turn, g):
        cols = pl.ds(pl.multiple_of(g * WIDE, WIDE), WIDE)
        return pltpu.make_async_copy(o.at[turn, g], out_ref.at[turn, :, cols], out_sem.at[turn, g])

    def lay_out(p):
        d1_copy(p).wait_recv()
        d2_copy(p).wait_recv()
        for m in range(3):
            parts = [w[p, v, m].astype(jnp.float32) for v in range(4)]
            dense[p // 4, m, p % 4] = jnp.concatenate(parts, axis=0).astype(jnp.bfloat16)

    def stream_copy(g, h):
        cols = pl.ds(h * HEAD, HEAD)
        return remote(
            o.at[0, g, :, cols], rs.at[0, g, :, cols], str_s.at[g, h], str_r.at[g, h], sec_hi
        )

    def send_stream(g, h):
        stream_copy(g, h).start()

    each_part = [(g, h) for g in range(GROUPS) for h in range(WIDE // HEAD)]

    near = jnp.where(z % 4 < 2, GROUPS - 1, 1)

    def group_at(k):
        base = z // 4
        step = jnp.where(k == 0, 0, jnp.where(k == 1, near, jnp.where(k == 2, GROUPS - near, 2)))
        return (base + step) % GROUPS

    def first_turn(k):
        g = group_at(k)
        project(0, g)
        attend(
            g, 0, lambda n: stale_other(g, n), lambda n: sl[g, n], lambda n: su[g, n],
            tile_rows(xb, g, j0), send_stream,
        )

    x_own()[1].wait_recv()
    for part in (2, 3):
        for way in range(2):
            z_copy(part, way, z).start()
    x_own()[0].wait_recv()
    d2_copy(z).start()

    def prepare():
        for cp in x_loads + st_loads + mod_loads:
            cp.wait()
        for cp in rims:
            cp.start()
        modulate([lambda g=g: tile_rows(xb, g, j0) for g in range(GROUPS)], 0, TILE)
        set_marks(0, j0)
        set_marks(1, 1 - j0)

        @pl.when(section == 0)
        def _():
            for g in range(GROUPS):
                rs[1, g] = tile_rows(xb, g, 1 - j0).astype(jnp.bfloat16)

    def neighbours():
        for cp in rims:
            cp.wait_recv()
        modulate([lambda g=g: pick(j0, xl[g], xu[g]) for g in range(GROUPS)], TILE, RIM)

    def ring_step(s, carry):
        before = plane(-s)
        after = plane(s)

        @pl.when(s <= 8)
        def _():
            z_wait(0, before)

            @pl.when(s <= 7)
            def _():
                z_copy(0, 0, before).start()

            x_start(before)

        @pl.when(s <= 7)
        def _():
            z_wait(0, after)

            @pl.when(s <= 6)
            def _():
                z_copy(0, 1, after).start()

            x_start(after)

        @pl.when(s >= 2)
        def _():
            p = plane(1 - s)
            x_wait(p)
            d2_copy(p).start()

        @pl.when((s >= 2) & (s <= 8))
        def _():
            p = plane(s - 1)
            x_wait(p)
            d2_copy(p).start()

        @pl.when(s <= 7)
        def _():
            for part in (1, 2, 3):
                z_wait(part, before)

                @pl.when(s <= 6)
                def _():
                    z_copy(part, 0, before).start()

            d1_copy(before).start()

        @pl.when(s <= 8)
        def _():
            for part in (1, 2, 3):
                z_wait(part, after)

                @pl.when(s <= 7)
                def _():
                    z_copy(part, 1, after).start()

            d1_copy(after).start()

        @pl.when(s == 1)
        def _():
            prepare()

        @pl.when(s == 3)
        def _():
            neighbours()

        lay_out(plane(1 - s))

        @pl.when((s >= 2) & (s <= 8))
        def _():
            lay_out(plane(s - 1))

        @pl.when((s == 4) | (s == 6) | (s >= 8))
        def _():
            first_turn(jnp.where(s == 9, 3, (s - 4) // 2))

        return carry

    lax.fori_loop(1, 10, ring_step, 0)

    for g, h in each_part:
        stream_copy(g, h).wait_recv()
    source = jnp.where(section == 0, 1, 0)
    modulate([lambda g=g: rs[source, g].astype(jnp.float32) for g in range(GROUPS)], 0, TILE)

    def second_turn(g, carry):
        project(1, g)
        attend(
            g, 1, lambda n: kv[1, g, n],
            lambda n: pick(j0, fr[g, n], sl[g, n]).astype(jnp.bfloat16),
            lambda n: pick(j0, su[g, n], fr[g, n]).astype(jnp.bfloat16),
            rs[source, g].astype(jnp.float32), lambda g, h: None,
        )
        return carry

    lax.fori_loop(0, GROUPS, second_turn, 0)

    for cp in x_own() + rims:
        cp.wait_send()
    for part in range(4):
        for way in range(2):
            z_copy(part, way, z).wait_send()
    d1_copy(z).wait_send()
    d2_copy(z).wait_send()
    for turn in range(2):
        for g in range(GROUPS):
            out_copy(turn, g).wait()

    for g, h in each_part:
        stream_copy(g, h).wait_send()

    def drain(s, carry):
        before = plane(-s)
        after = plane(s)
        z_copy(0, 0, before).wait_send()
        x_drain(before)
        d1_copy(before).wait_send()
        d2_copy(before).wait_send()
        for part in (1, 2, 3):
            z_copy(part, 1, after).wait_send()

        @pl.when(s <= 6)
        def _():
            z_copy(0, 1, after).wait_send()
            for part in (1, 2, 3):
                z_copy(part, 0, before).wait_send()

        x_drain(after)
        d1_copy(after).wait_send()
        d2_copy(after).wait_send()
        return carry

    lax.fori_loop(1, 8, drain, 0)
    far = plane(8)
    x_drain(far)
    d1_copy(far).wait_send()
    d2_copy(far).wait_send()


def shards(block_inputs, stale_kv, projection, modulation, pattern, order):
    dma = pltpu.SemaphoreType.DMA
    vmem = pltpu.VMEM
    bf16 = jnp.bfloat16
    out = pl.pallas_call(
        kernel,
        out_shape=jax.ShapeDtypeStruct((2, TILE, FEAT), bf16),
        in_specs=[pl.BlockSpec(memory_space=pl.ANY)] * 4
        + [pl.BlockSpec(memory_space=pltpu.VMEM)] * 2,
        out_specs=pl.BlockSpec(memory_space=pl.ANY),
        scratch_shapes=[
            vmem((PLANES, 4, 3, COLS, FEAT), bf16),
            vmem((GROUPS, 3, 4, 4 * COLS, FEAT), bf16),
            vmem((GROUPS, 2 * TILE, WIDE), bf16),
            vmem((GROUPS, 2, 2 * TILE, WIDE), bf16),
            vmem((TILE + RIM, FEAT), bf16),
            vmem((GROUPS, TILE, WIDE), bf16),
            vmem((2, GROUPS, 2, TILE, WIDE), bf16),
            vmem((2, GROUPS, TILE, WIDE), bf16),
            vmem((2, GROUPS, TILE, WIDE), bf16),
            vmem((GROUPS, 2, RIM, WIDE), bf16),
            vmem((GROUPS, 2, RIM, WIDE), bf16),
            vmem((GROUPS, RIM, WIDE), bf16),
            vmem((GROUPS, RIM, WIDE), bf16),
            vmem((GROUPS, 2, RIM, WIDE), bf16),
            vmem((2, WINDOW, HEAD), bf16),
            vmem((8, FEAT), jnp.float32),
            dma((16,)),
            dma((4, 2, PLANES)),
            dma((4, PLANES)),
            dma((2, PLANES)),
            dma((2, PLANES)),
            dma((PLANES,)),
            dma((PLANES,)),
            dma((PLANES,)),
            dma((PLANES,)),
            dma((4,)),
            dma((4,)),
            dma((GROUPS, WIDE // HEAD)),
            dma((GROUPS, WIDE // HEAD)),
            dma((2, GROUPS)),
        ],
        compiler_params=pltpu.CompilerParams(
            collective_id=0, has_side_effects=True, vmem_limit_bytes=58 * 2**20
        ),
        name="blocks",
    )(
        block_inputs[0],
        stale_kv[0],
        jnp.swapaxes(projection[0], 1, 2),
        jnp.swapaxes(modulation, 0, 1),
        pattern,
        order.reshape(1, 2),
    )
    swapped = order[lax.axis_index("section") % 2] > 0
    placed = jnp.where(swapped, out[::-1], out)
    return placed.reshape(1, 2 * TILE, FEAT)


def solution(mesh):
    placed = (
        P("section", "tile", None),
        P("section", "tile", None),
        P("section", None, None, "tile"),
        P("section", None, None),
        P("tile", None),
        P(),
    )
    return jax.shard_map(
        shards, mesh=mesh, in_specs=placed, out_specs=P("section", "tile", None), check_vma=False
    )
```

```python
import math

import jax
import jax.numpy as jnp
from jax import lax
from jax.experimental import pallas as pl
from jax.experimental.pallas import tpu as pltpu
from jax.sharding import PartitionSpec as P

HEADS = 12
FEAT = 1536
TILE = 192
RIM = 48
PLANES = 16
SECTIONS = 8
TILES = 64
COLS = 24
GROUPS = 4
WIDE = FEAT // GROUPS
HEAD = FEAT // HEADS
WINDOW = 2 * TILE + 2 * RIM
DUP = 768
EPS = 1e-06
MESH = pl.DeviceIdType.MESH
NT = (((1,), (1,)), ((), ()))
SCALE = math.log2(math.e) / math.sqrt(HEAD)


def kernel(
    x_hbm, stale_hbm, proj_hbm, mod_hbm, pattern_ref, order_ref, out_ref,
    w, dense, turned, stage, xb, st, hidden, q, kv, o, rs, sl, su, xl, xu, fr, marks, mod_ref,
    loc_sem, zs, zr, xs, xr, d1s, d1r, d2s, d2r, rim_s, rim_r, str_s, str_r, out_sem,
):
    section = lax.axis_index("section")
    tile = lax.axis_index("tile")
    z = tile // 4
    xh = (tile // 2) % 2
    c = tile % 2
    u = xh * 2 + c
    up = (1 - xh) * 2 + c

    def plane(d):
        return (z + d + PLANES) % PLANES

    def at_tile(t):
        return (section, t)

    z_dev = (
        at_tile(((z + 1) % PLANES) * 4 + u),
        at_tile(((z + PLANES - 1) % PLANES) * 4 + u),
    )
    x_dev = at_tile(z * 4 + up)
    sib = at_tile(z * 4 + xh * 2 + (1 - c))
    tile_hi = at_tile((tile + 1) % TILES)
    tile_lo = at_tile((tile + TILES - 1) % TILES)
    sec_hi = ((section + 1) % SECTIONS, tile)
    sec_lo = ((section + SECTIONS - 1) % SECTIONS, tile)

    own_w = pltpu.make_async_copy(proj_hbm, w.at[z, u], loc_sem.at[0])
    own_w.start()
    x_loads = [
        pltpu.make_async_copy(x_hbm.at[:, pl.ds(g * WIDE, WIDE)], xb.at[g], loc_sem.at[1 + g])
        for g in range(GROUPS)
    ]
    st_loads = [
        pltpu.make_async_copy(
            stale_hbm.at[:, pl.ds((k * GROUPS + g) * WIDE, WIDE)], st.at[g, k],
            loc_sem.at[5 + 2 * g + k],
        )
        for g in range(GROUPS)
        for k in range(2)
    ]
    mod_loads = [
        pltpu.make_async_copy(mod_hbm.at[m], mod_ref.at[pl.ds(m, 1)], loc_sem.at[13 + m])
        for m in range(3)
    ]
    for cp in x_loads + st_loads + mod_loads:
        cp.start()

    bar = pltpu.get_barrier_semaphore()
    peers = (z_dev[0], z_dev[1], x_dev, sib, tile_hi, tile_lo, sec_hi, sec_lo)
    for dev in peers:
        pl.semaphore_signal(bar, inc=1, device_id=dev, device_id_type=MESH)
    pl.semaphore_wait(bar, len(peers))

    def remote(src, dst, s, r, dev):
        return pltpu.make_async_remote_copy(
            src_ref=src, dst_ref=dst, send_sem=s, recv_sem=r, device_id=dev, device_id_type=MESH
        )

    def z_copy(part, way, p):
        if part == 0:
            ref = w.at[p, u, pl.ds(0, 2)]
        elif part == 1:
            ref = w.at[p, u, 2]
        elif part == 2:
            ref = w.at[p, up, 2]
        else:
            ref = w.at[p, up, 1, :, pl.ds(0, DUP)]
        return remote(ref, ref, zs.at[part, way, p], zr.at[part, p], z_dev[way])

    def z_wait(part, p):
        z_copy(part, 0, p).wait_recv()

    def x_copies(p):
        refs = (w.at[p, u, 0], w.at[p, u, 1, :, pl.ds(DUP, FEAT - DUP)])
        return [
            remote(ref, ref, xs.at[i, p], xr.at[i, p], x_dev) for i, ref in enumerate(refs)
        ]

    def x_own():
        refs = (w.at[z, u, 0], w.at[z, u, pl.ds(1, 2)])
        return [
            remote(ref, ref, xs.at[i, z], xr.at[i, z], x_dev) for i, ref in enumerate(refs)
        ]

    def x_start(p):
        for cp in x_copies(p):
            cp.start()

    def x_wait(p):
        for cp in x_copies(p):
            cp.wait_recv()

    def x_drain(p):
        for cp in x_copies(p):
            cp.wait_send()

    def d1_copy(p):
        ref = w.at[p, u]
        return remote(ref, ref, d1s.at[p], d1r.at[p], sib)

    def d2_copy(p):
        ref = w.at[p, up]
        return remote(ref, ref, d2s.at[p], d2r.at[p], sib)

    own_w.wait()
    x_own()[1].start()
    x_own()[0].start()
    for part in (0, 1):
        for way in range(2):
            z_copy(part, way, z).start()
    d1_copy(z).start()

    head_rows = pl.ds(0, RIM)
    tail_rows = pl.ds(2 * TILE - RIM, RIM)
    rims = [
        remote(st.at[:, :, head_rows, :], su, rim_s.at[0], rim_r.at[0], tile_lo),
        remote(st.at[:, :, tail_rows, :], sl, rim_s.at[1], rim_r.at[1], tile_hi),
        remote(xb.at[:, head_rows, :], xu, rim_s.at[2], rim_r.at[2], tile_lo),
        remote(xb.at[:, tail_rows, :], xl, rim_s.at[3], rim_r.at[3], tile_hi),
    ]

    parity = section % 2
    first = order_ref[0:1, 0:1]
    second = order_ref[0:1, 1:2]
    j0 = jnp.where(parity == 0, first, second)
    has_lo = jnp.where(tile > 0, 1, 0)
    has_hi = jnp.where(tile < TILES - 1, 1, 0)

    def pick(flag, yes, no):
        on = jnp.broadcast_to(flag, yes.shape) > 0
        return jnp.where(on, yes.astype(jnp.float32), no.astype(jnp.float32))

    def set_marks(turn, j):
        def mark(slot):
            one, two = pattern_ref[0:1, slot : slot + 1], pattern_ref[1:2, slot : slot + 1]
            return one + j * (two - one)

        one, two = mark(1), mark(2)
        spans = (
            (one + j0 * (two - one), TILE),
            (two + j0 * (one - two), TILE),
            (mark(0) * has_lo, RIM),
            (mark(3) * has_hi, RIM),
        )
        start = 0
        for value, width in spans:
            on = jnp.broadcast_to(value, (width, HEAD)) > 0
            marks[turn, pl.ds(start, width), :] = jnp.where(on, 1.0, 0.0).astype(jnp.bfloat16)
            start += width

    def tile_rows(ref, g, j):
        return pick(j, ref[g, TILE : 2 * TILE, :], ref[g, 0:TILE, :])

    def stale_other(g, n):
        one, two = st[g, n, 0:TILE, :], st[g, n, TILE : 2 * TILE, :]
        return pick(j0, one, two).astype(jnp.bfloat16)

    def modulate(parts, start, count):
        total = jnp.zeros((count, 1), jnp.float32)
        for part in parts:
            values = part()
            total = total + jnp.sum(values * values, axis=1, keepdims=True)
        inv = lax.rsqrt(total * (1.0 / FEAT) + EPS)
        for g, part in enumerate(parts):
            cols = pl.ds(g * WIDE, WIDE)
            normed = part() * inv
            hidden[pl.ds(start, count), cols] = (
                (1.0 + mod_ref[1:2, cols]) * normed + mod_ref[0:1, cols]
            ).astype(jnp.bfloat16)

    def head_norm(rows, factor):
        parts = []
        for h in range(WIDE // HEAD):
            one = rows[:, h * HEAD : (h + 1) * HEAD]
            mean = jnp.mean(one * one, axis=1, keepdims=True)
            parts.append(one * (lax.rsqrt(mean + EPS) * factor))
        return jnp.concatenate(parts, axis=1).astype(jnp.bfloat16)

    def turn_weights(g):
        for m in range(3):
            turned[g, :, m * WIDE : (m + 1) * WIDE] = dense[g, m].reshape(WIDE, FEAT).T

    def project_again(g):
        res = jnp.dot(
            hidden[pl.ds(0, TILE), :], turned[g], preferred_element_type=jnp.float32
        )
        q[g] = head_norm(res[:, 0:WIDE], SCALE)
        kv[1, g, 0] = head_norm(res[:, WIDE : 2 * WIDE], 1.0)
        kv[1, g, 1] = res[:, 2 * WIDE : 3 * WIDE].astype(jnp.bfloat16)

    def project(g):
        count = TILE + RIM
        rows = hidden[pl.ds(0, count), :]
        for m in range(3):
            weight = dense[g, m].reshape(WIDE, FEAT)
            res = lax.dot_general(
                rows if m else rows[0:TILE], weight, NT, preferred_element_type=jnp.float32
            )
            low = head_norm(res, 1.0 if m else SCALE) if m < 2 else res.astype(jnp.bfloat16)
            if m == 0:
                q[g] = low
                continue
            kv[0, g, m - 1] = low[0:TILE]
            fr[g, m - 1] = low[TILE:count]

    def attend(g, turn, other, low, high, stream, ready):
        def window(k):
            return jnp.concatenate([kv[0, g, k], other(k), low(k), high(k)], axis=0)

        keys = window(0)
        values = window(1)
        queries = q[g]
        mark = marks[turn]
        gate = mod_ref[2:3, pl.ds(pl.multiple_of(g * WIDE, WIDE), WIDE)]
        for h in range(WIDE // HEAD):
            cols = slice(h * HEAD, (h + 1) * HEAD)
            scores = lax.dot_general(
                queries[:, cols], keys[:, cols], NT, preferred_element_type=jnp.float32
            )
            unnormed = jnp.exp2(scores).astype(jnp.bfloat16)
            marked = jnp.concatenate([values[:, cols] * mark, mark], axis=1)
            both = jnp.dot(unnormed, marked, preferred_element_type=jnp.float32)
            attended = both[:, :HEAD] / both[:, HEAD:]
            o[turn, g, :, cols] = (stream[:, cols] + gate[:, cols] * attended).astype(jnp.bfloat16)
            ready(g, h)

    def out_copy(j, g):
        rows = pl.ds(j * TILE, TILE)
        cols = pl.ds(pl.multiple_of(g * WIDE, WIDE), WIDE)
        return pltpu.make_async_copy(stage.at[j, g], out_ref.at[rows, cols], out_sem.at[j, g])

    def put_out(g):
        early, late = o[0, g], o[1, g]
        stage[0, g] = pick(j0, late, early).astype(jnp.bfloat16)
        stage[1, g] = pick(j0, early, late).astype(jnp.bfloat16)
        for j in range(2):
            out_copy(j, g).start()

    def lay_out(p):
        d1_copy(p).wait_recv()
        d2_copy(p).wait_recv()
        for m in range(3):
            parts = [w[p, v, m].astype(jnp.float32) for v in range(4)]
            dense[p // 4, m, p % 4] = jnp.concatenate(parts, axis=0).astype(jnp.bfloat16)

    def stream_copy(g, h):
        cols = pl.ds(h * HEAD, HEAD)
        return remote(
            o.at[0, g, :, cols], rs.at[0, g, :, cols], str_s.at[g, h], str_r.at[g, h], sec_hi
        )

    def send_stream(g, h):
        stream_copy(g, h).start()

    each_part = [(g, h) for g in range(GROUPS) for h in range(WIDE // HEAD)]

    near = jnp.where(z % 4 < 2, GROUPS - 1, 1)

    def group_at(k):
        base = z // 4
        step = jnp.where(k == 0, 0, jnp.where(k == 1, near, jnp.where(k == 2, GROUPS - near, 2)))
        return (base + step) % GROUPS

    def first_turn(k):
        g = group_at(k)
        project(g)
        attend(
            g, 0, lambda n: stale_other(g, n), lambda n: sl[g, n], lambda n: su[g, n],
            tile_rows(xb, g, j0), send_stream,
        )

    x_own()[1].wait_recv()
    for part in (2, 3):
        for way in range(2):
            z_copy(part, way, z).start()
    x_own()[0].wait_recv()
    d2_copy(z).start()

    def prepare():
        for cp in x_loads + st_loads + mod_loads:
            cp.wait()
        for cp in rims:
            cp.start()
        modulate([lambda g=g: tile_rows(xb, g, j0) for g in range(GROUPS)], 0, TILE)
        set_marks(0, j0)
        set_marks(1, 1 - j0)

        @pl.when(section == 0)
        def _():
            for g in range(GROUPS):
                rs[1, g] = tile_rows(xb, g, 1 - j0).astype(jnp.bfloat16)

    def neighbours():
        for cp in rims:
            cp.wait_recv()
        modulate([lambda g=g: pick(j0, xl[g], xu[g]) for g in range(GROUPS)], TILE, RIM)

    def ring_step(s, carry):
        before = plane(-s)
        after = plane(s)

        @pl.when(s <= 8)
        def _():
            z_wait(0, before)

            @pl.when(s <= 7)
            def _():
                z_copy(0, 0, before).start()

            x_start(before)

        @pl.when(s <= 7)
        def _():
            z_wait(0, after)

            @pl.when(s <= 6)
            def _():
                z_copy(0, 1, after).start()

            x_start(after)

        @pl.when(s >= 2)
        def _():
            p = plane(1 - s)
            x_wait(p)
            d2_copy(p).start()

        @pl.when((s >= 2) & (s <= 8))
        def _():
            p = plane(s - 1)
            x_wait(p)
            d2_copy(p).start()

        @pl.when(s <= 7)
        def _():
            for part in (1, 2, 3):
                z_wait(part, before)

                @pl.when(s <= 6)
                def _():
                    z_copy(part, 0, before).start()

            d1_copy(before).start()

        @pl.when(s <= 8)
        def _():
            for part in (1, 2, 3):
                z_wait(part, after)

                @pl.when(s <= 7)
                def _():
                    z_copy(part, 1, after).start()

            d1_copy(after).start()

        @pl.when(s == 1)
        def _():
            prepare()

        @pl.when(s == 3)
        def _():
            neighbours()

        lay_out(plane(1 - s))

        @pl.when((s >= 2) & (s <= 8))
        def _():
            lay_out(plane(s - 1))

        @pl.when((s == 4) | (s == 6) | (s >= 8))
        def _():
            first_turn(jnp.where(s == 9, 3, (s - 4) // 2))

        @pl.when((s == 5) | (s == 7))
        def _():
            turn_weights(group_at((s - 5) // 2))

        return carry

    lax.fori_loop(1, 10, ring_step, 0)

    def last_turned(k, carry):
        turn_weights(group_at(k))
        return carry

    lax.fori_loop(2, GROUPS, last_turned, 0)
    for g, h in each_part:
        stream_copy(g, h).wait_recv()
    source = jnp.where(section == 0, 1, 0)
    modulate([lambda g=g: rs[source, g].astype(jnp.float32) for g in range(GROUPS)], 0, TILE)

    def second_turn(g, carry):
        project_again(g)
        attend(
            g, 1, lambda n: kv[1, g, n],
            lambda n: pick(j0, fr[g, n], sl[g, n]).astype(jnp.bfloat16),
            lambda n: pick(j0, su[g, n], fr[g, n]).astype(jnp.bfloat16),
            rs[source, g].astype(jnp.float32), lambda g, h: None,
        )
        put_out(g)
        return carry

    lax.fori_loop(0, GROUPS, second_turn, 0)

    for cp in x_own() + rims:
        cp.wait_send()
    for part in range(4):
        for way in range(2):
            z_copy(part, way, z).wait_send()
    d1_copy(z).wait_send()
    d2_copy(z).wait_send()
    for j in range(2):
        for g in range(GROUPS):
            out_copy(j, g).wait()

    for g, h in each_part:
        stream_copy(g, h).wait_send()

    def drain(s, carry):
        before = plane(-s)
        after = plane(s)
        z_copy(0, 0, before).wait_send()
        x_drain(before)
        d1_copy(before).wait_send()
        d2_copy(before).wait_send()
        for part in (1, 2, 3):
            z_copy(part, 1, after).wait_send()

        @pl.when(s <= 6)
        def _():
            z_copy(0, 1, after).wait_send()
            for part in (1, 2, 3):
                z_copy(part, 0, before).wait_send()

        x_drain(after)
        d1_copy(after).wait_send()
        d2_copy(after).wait_send()
        return carry

    lax.fori_loop(1, 8, drain, 0)
    far = plane(8)
    x_drain(far)
    d1_copy(far).wait_send()
    d2_copy(far).wait_send()


def shards(block_inputs, stale_kv, projection, modulation, pattern, order):
    dma = pltpu.SemaphoreType.DMA
    vmem = pltpu.VMEM
    bf16 = jnp.bfloat16
    out = pl.pallas_call(
        kernel,
        out_shape=jax.ShapeDtypeStruct((2 * TILE, FEAT), bf16),
        in_specs=[pl.BlockSpec(memory_space=pl.ANY)] * 4
        + [pl.BlockSpec(memory_space=pltpu.VMEM)] * 2,
        out_specs=pl.BlockSpec(memory_space=pl.ANY),
        scratch_shapes=[
            vmem((PLANES, 4, 3, COLS, FEAT), bf16),
            vmem((GROUPS, 3, 4, 4 * COLS, FEAT), bf16),
            vmem((GROUPS, FEAT, 3 * WIDE), bf16),
            vmem((2, GROUPS, TILE, WIDE), bf16),
            vmem((GROUPS, 2 * TILE, WIDE), bf16),
            vmem((GROUPS, 2, 2 * TILE, WIDE), bf16),
            vmem((TILE + RIM, FEAT), bf16),
            vmem((GROUPS, TILE, WIDE), bf16),
            vmem((2, GROUPS, 2, TILE, WIDE), bf16),
            vmem((2, GROUPS, TILE, WIDE), bf16),
            vmem((2, GROUPS, TILE, WIDE), bf16),
            vmem((GROUPS, 2, RIM, WIDE), bf16),
            vmem((GROUPS, 2, RIM, WIDE), bf16),
            vmem((GROUPS, RIM, WIDE), bf16),
            vmem((GROUPS, RIM, WIDE), bf16),
            vmem((GROUPS, 2, RIM, WIDE), bf16),
            vmem((2, WINDOW, HEAD), bf16),
            vmem((8, FEAT), jnp.float32),
            dma((16,)),
            dma((4, 2, PLANES)),
            dma((4, PLANES)),
            dma((2, PLANES)),
            dma((2, PLANES)),
            dma((PLANES,)),
            dma((PLANES,)),
            dma((PLANES,)),
            dma((PLANES,)),
            dma((4,)),
            dma((4,)),
            dma((GROUPS, WIDE // HEAD)),
            dma((GROUPS, WIDE // HEAD)),
            dma((2, GROUPS)),
        ],
        compiler_params=pltpu.CompilerParams(
            collective_id=0, has_side_effects=True, vmem_limit_bytes=58 * 2**20
        ),
        name="blocks",
    )(
        block_inputs[0],
        stale_kv[0],
        jnp.swapaxes(projection[0], 1, 2),
        jnp.swapaxes(modulation, 0, 1),
        pattern,
        order.reshape(1, 2),
    )
    return out[None]


def solution(mesh):
    placed = (
        P("section", "tile", None),
        P("section", "tile", None),
        P("section", None, None, "tile"),
        P("section", None, None),
        P("tile", None),
        P(),
    )
    return jax.shard_map(
        shards, mesh=mesh, in_specs=placed, out_specs=P("section", "tile", None), check_vma=False
    )
```

```python
import math

import jax
import jax.numpy as jnp
from jax import lax
from jax.experimental import pallas as pl
from jax.experimental.pallas import tpu as pltpu
from jax.sharding import PartitionSpec as P

HEADS = 12
FEAT = 1536
TILE = 192
RIM = 48
PLANES = 16
SECTIONS = 8
TILES = 64
COLS = 24
GROUPS = 4
WIDE = FEAT // GROUPS
HEAD = FEAT // HEADS
WINDOW = 2 * TILE + 2 * RIM
DUP = 768
EPS = 1e-06
MESH = pl.DeviceIdType.MESH
NT = (((1,), (1,)), ((), ()))
SCALE = math.log2(math.e) / math.sqrt(HEAD)


def kernel(
    x_hbm, stale_hbm, proj_hbm, mod_hbm, pattern_ref, order_ref, out_ref,
    w, dense, turned, xb, st, hidden, q, kv, o, rs, sl, su, xl, xu, fr, marks, mod_ref,
    loc_sem, zs, zr, xs, xr, d1s, d1r, d2s, d2r, rim_s, rim_r, str_s, str_r,
):
    section = lax.axis_index("section")
    tile = lax.axis_index("tile")
    z = tile // 4
    xh = (tile // 2) % 2
    c = tile % 2
    u = xh * 2 + c
    up = (1 - xh) * 2 + c

    def plane(d):
        return (z + d + PLANES) % PLANES

    def at_tile(t):
        return (section, t)

    z_dev = (
        at_tile(((z + 1) % PLANES) * 4 + u),
        at_tile(((z + PLANES - 1) % PLANES) * 4 + u),
    )
    x_dev = at_tile(z * 4 + up)
    sib = at_tile(z * 4 + xh * 2 + (1 - c))
    tile_hi = at_tile((tile + 1) % TILES)
    tile_lo = at_tile((tile + TILES - 1) % TILES)
    sec_hi = ((section + 1) % SECTIONS, tile)
    sec_lo = ((section + SECTIONS - 1) % SECTIONS, tile)

    own_w = pltpu.make_async_copy(proj_hbm, w.at[z, u], loc_sem.at[0])
    own_w.start()
    x_loads = [
        pltpu.make_async_copy(x_hbm.at[:, pl.ds(g * WIDE, WIDE)], xb.at[g], loc_sem.at[1 + g])
        for g in range(GROUPS)
    ]
    st_loads = [
        pltpu.make_async_copy(
            stale_hbm.at[:, pl.ds((k * GROUPS + g) * WIDE, WIDE)], st.at[g, k],
            loc_sem.at[5 + 2 * g + k],
        )
        for g in range(GROUPS)
        for k in range(2)
    ]
    mod_loads = [
        pltpu.make_async_copy(mod_hbm.at[m], mod_ref.at[pl.ds(m, 1)], loc_sem.at[13 + m])
        for m in range(3)
    ]
    for cp in x_loads + st_loads + mod_loads:
        cp.start()

    bar = pltpu.get_barrier_semaphore()
    peers = (z_dev[0], z_dev[1], x_dev, sib, tile_hi, tile_lo, sec_hi, sec_lo)
    for dev in peers:
        pl.semaphore_signal(bar, inc=1, device_id=dev, device_id_type=MESH)
    pl.semaphore_wait(bar, len(peers))

    def remote(src, dst, s, r, dev):
        return pltpu.make_async_remote_copy(
            src_ref=src, dst_ref=dst, send_sem=s, recv_sem=r, device_id=dev, device_id_type=MESH
        )

    def z_copy(part, way, p):
        if part == 0:
            ref = w.at[p, u, pl.ds(0, 2)]
        elif part == 1:
            ref = w.at[p, u, 2]
        elif part == 2:
            ref = w.at[p, up, 2]
        else:
            ref = w.at[p, up, 1, :, pl.ds(0, DUP)]
        return remote(ref, ref, zs.at[part, way, p], zr.at[part, p], z_dev[way])

    def z_wait(part, p):
        z_copy(part, 0, p).wait_recv()

    def x_copies(p):
        refs = (w.at[p, u, 0], w.at[p, u, 1, :, pl.ds(DUP, FEAT - DUP)])
        return [
            remote(ref, ref, xs.at[i, p], xr.at[i, p], x_dev) for i, ref in enumerate(refs)
        ]

    def x_own():
        refs = (w.at[z, u, 0], w.at[z, u, pl.ds(1, 2)])
        return [
            remote(ref, ref, xs.at[i, z], xr.at[i, z], x_dev) for i, ref in enumerate(refs)
        ]

    def x_start(p):
        for cp in x_copies(p):
            cp.start()

    def x_wait(p):
        for cp in x_copies(p):
            cp.wait_recv()

    def x_drain(p):
        for cp in x_copies(p):
            cp.wait_send()

    def d1_copy(p):
        ref = w.at[p, u]
        return remote(ref, ref, d1s.at[p], d1r.at[p], sib)

    def d2_copy(p):
        ref = w.at[p, up]
        return remote(ref, ref, d2s.at[p], d2r.at[p], sib)

    own_w.wait()
    x_own()[1].start()
    x_own()[0].start()
    for part in (0, 1):
        for way in range(2):
            z_copy(part, way, z).start()
    d1_copy(z).start()

    head_rows = pl.ds(0, RIM)
    tail_rows = pl.ds(2 * TILE - RIM, RIM)
    rims = [
        remote(st.at[:, :, head_rows, :], su, rim_s.at[0], rim_r.at[0], tile_lo),
        remote(st.at[:, :, tail_rows, :], sl, rim_s.at[1], rim_r.at[1], tile_hi),
        remote(xb.at[:, head_rows, :], xu, rim_s.at[2], rim_r.at[2], tile_lo),
        remote(xb.at[:, tail_rows, :], xl, rim_s.at[3], rim_r.at[3], tile_hi),
    ]

    parity = section % 2
    first = order_ref[0:1, 0:1]
    second = order_ref[0:1, 1:2]
    j0 = jnp.where(parity == 0, first, second)
    has_lo = jnp.where(tile > 0, 1, 0)
    has_hi = jnp.where(tile < TILES - 1, 1, 0)

    def pick(flag, yes, no):
        on = jnp.broadcast_to(flag, yes.shape) > 0
        return jnp.where(on, yes.astype(jnp.float32), no.astype(jnp.float32))

    def set_marks(turn, j):
        def mark(slot):
            one, two = pattern_ref[0:1, slot : slot + 1], pattern_ref[1:2, slot : slot + 1]
            return one + j * (two - one)

        one, two = mark(1), mark(2)
        spans = (
            (one + j0 * (two - one), TILE),
            (two + j0 * (one - two), TILE),
            (mark(0) * has_lo, RIM),
            (mark(3) * has_hi, RIM),
        )
        start = 0
        for value, width in spans:
            on = jnp.broadcast_to(value, (width, HEAD)) > 0
            marks[turn, pl.ds(start, width), :] = jnp.where(on, 1.0, 0.0).astype(jnp.bfloat16)
            start += width

    def tile_rows(ref, g, j):
        return pick(j, ref[g, TILE : 2 * TILE, :], ref[g, 0:TILE, :])

    def stale_other(g, n):
        one, two = st[g, n, 0:TILE, :], st[g, n, TILE : 2 * TILE, :]
        return pick(j0, one, two).astype(jnp.bfloat16)

    def modulate(parts, start, count):
        total = jnp.zeros((count, 1), jnp.float32)
        for part in parts:
            values = part()
            total = total + jnp.sum(values * values, axis=1, keepdims=True)
        inv = lax.rsqrt(total * (1.0 / FEAT) + EPS)
        for g, part in enumerate(parts):
            cols = pl.ds(g * WIDE, WIDE)
            normed = part() * inv
            hidden[pl.ds(start, count), cols] = (
                (1.0 + mod_ref[1:2, cols]) * normed + mod_ref[0:1, cols]
            ).astype(jnp.bfloat16)

    def head_norm(rows, factor):
        parts = []
        for h in range(WIDE // HEAD):
            one = rows[:, h * HEAD : (h + 1) * HEAD]
            mean = jnp.mean(one * one, axis=1, keepdims=True)
            parts.append(one * (lax.rsqrt(mean + EPS) * factor))
        return jnp.concatenate(parts, axis=1).astype(jnp.bfloat16)

    def turn_weights(g):
        for m in range(3):
            turned[g, :, m * WIDE : (m + 1) * WIDE] = dense[g, m].reshape(WIDE, FEAT).T

    def project_again(g):
        res = jnp.dot(
            hidden[pl.ds(0, TILE), :], turned[g], preferred_element_type=jnp.float32
        )
        q[g] = head_norm(res[:, 0:WIDE], SCALE)
        kv[1, g, 0] = head_norm(res[:, WIDE : 2 * WIDE], 1.0)
        kv[1, g, 1] = res[:, 2 * WIDE : 3 * WIDE].astype(jnp.bfloat16)

    def project(g):
        count = TILE + RIM
        rows = hidden[pl.ds(0, count), :]
        for m in range(3):
            weight = dense[g, m].reshape(WIDE, FEAT)
            res = lax.dot_general(
                rows if m else rows[0:TILE], weight, NT, preferred_element_type=jnp.float32
            )
            low = head_norm(res, 1.0 if m else SCALE) if m < 2 else res.astype(jnp.bfloat16)
            if m == 0:
                q[g] = low
                continue
            kv[0, g, m - 1] = low[0:TILE]
            fr[g, m - 1] = low[TILE:count]

    def columns_of(g):
        start = g * WIDE
        return pl.ds(start if isinstance(g, int) else pl.multiple_of(start, WIDE), WIDE)

    def attend(g, turn, other, low, high, stream, ready):
        def window(k):
            return jnp.concatenate([kv[0, g, k], other(k), low(k), high(k)], axis=0)

        keys = window(0)
        values = window(1)
        queries = q[g]
        mark = marks[turn]
        gate = mod_ref[2:3, columns_of(g)]
        for h in range(WIDE // HEAD):
            cols = slice(h * HEAD, (h + 1) * HEAD)
            scores = lax.dot_general(
                queries[:, cols], keys[:, cols], NT, preferred_element_type=jnp.float32
            )
            unnormed = jnp.exp2(scores).astype(jnp.bfloat16)
            marked = jnp.concatenate([values[:, cols] * mark, mark], axis=1)
            both = jnp.dot(unnormed, marked, preferred_element_type=jnp.float32)
            attended = both[:, :HEAD] / both[:, HEAD:]
            o[turn, g, :, cols] = (stream[:, cols] + gate[:, cols] * attended).astype(jnp.bfloat16)
            ready(g, h)

    def put_out(g):
        early, late = o[0, g], o[1, g]
        cols = pl.ds(g * WIDE, WIDE)
        out_ref[pl.ds(0, TILE), cols] = pick(j0, late, early).astype(jnp.bfloat16)
        out_ref[pl.ds(TILE, TILE), cols] = pick(j0, early, late).astype(jnp.bfloat16)

    def lay_out(p):
        d1_copy(p).wait_recv()
        d2_copy(p).wait_recv()
        for m in range(3):
            parts = [w[p, v, m].astype(jnp.float32) for v in range(4)]
            dense[p // 4, m, p % 4] = jnp.concatenate(parts, axis=0).astype(jnp.bfloat16)

    def stream_copy(g, h):
        cols = pl.ds(h * HEAD, HEAD)
        return remote(
            o.at[0, g, :, cols], rs.at[0, g, :, cols], str_s.at[g, h], str_r.at[g, h], sec_hi
        )

    def send_stream(g, h):
        stream_copy(g, h).start()

    each_part = [(g, h) for g in range(GROUPS) for h in range(WIDE // HEAD)]

    near = jnp.where(z % 4 < 2, GROUPS - 1, 1)

    def group_at(k):
        base = z // 4
        step = jnp.where(k == 0, 0, jnp.where(k == 1, near, jnp.where(k == 2, GROUPS - near, 2)))
        return (base + step) % GROUPS

    def first_turn(k):
        g = group_at(k)
        project(g)
        attend(
            g, 0, lambda n: stale_other(g, n), lambda n: sl[g, n], lambda n: su[g, n],
            tile_rows(xb, g, j0), send_stream,
        )

    x_own()[1].wait_recv()
    for part in (2, 3):
        for way in range(2):
            z_copy(part, way, z).start()
    x_own()[0].wait_recv()
    d2_copy(z).start()

    def prepare():
        for cp in x_loads + st_loads + mod_loads:
            cp.wait()
        for cp in rims:
            cp.start()
        modulate([lambda g=g: tile_rows(xb, g, j0) for g in range(GROUPS)], 0, TILE)
        set_marks(0, j0)
        set_marks(1, 1 - j0)

        @pl.when(section == 0)
        def _():
            for g in range(GROUPS):
                rs[1, g] = tile_rows(xb, g, 1 - j0).astype(jnp.bfloat16)

    def neighbours():
        for cp in rims:
            cp.wait_recv()
        modulate([lambda g=g: pick(j0, xl[g], xu[g]) for g in range(GROUPS)], TILE, RIM)

    def ring_step(s, carry):
        before = plane(-s)
        after = plane(s)

        @pl.when(s <= 8)
        def _():
            z_wait(0, before)

            @pl.when(s <= 7)
            def _():
                z_copy(0, 0, before).start()

            x_start(before)

        @pl.when(s <= 7)
        def _():
            z_wait(0, after)

            @pl.when(s <= 6)
            def _():
                z_copy(0, 1, after).start()

            x_start(after)

        @pl.when(s >= 2)
        def _():
            p = plane(1 - s)
            x_wait(p)
            d2_copy(p).start()

        @pl.when((s >= 2) & (s <= 8))
        def _():
            p = plane(s - 1)
            x_wait(p)
            d2_copy(p).start()

        @pl.when(s <= 7)
        def _():
            for part in (1, 2, 3):
                z_wait(part, before)

                @pl.when(s <= 6)
                def _():
                    z_copy(part, 0, before).start()

            d1_copy(before).start()

        @pl.when(s <= 8)
        def _():
            for part in (1, 2, 3):
                z_wait(part, after)

                @pl.when(s <= 7)
                def _():
                    z_copy(part, 1, after).start()

            d1_copy(after).start()

        @pl.when(s == 1)
        def _():
            prepare()

        @pl.when(s == 3)
        def _():
            neighbours()

        lay_out(plane(1 - s))

        @pl.when((s >= 2) & (s <= 8))
        def _():
            lay_out(plane(s - 1))

        @pl.when((s == 4) | (s == 6) | (s >= 8))
        def _():
            first_turn(jnp.where(s == 9, 3, (s - 4) // 2))

        @pl.when((s == 5) | (s == 7))
        def _():
            turn_weights(group_at((s - 5) // 2))

        return carry

    lax.fori_loop(1, 10, ring_step, 0)

    def last_turned(k, carry):
        turn_weights(group_at(k))
        return carry

    lax.fori_loop(2, GROUPS, last_turned, 0)
    for g, h in each_part:
        stream_copy(g, h).wait_recv()
    source = jnp.where(section == 0, 1, 0)
    modulate([lambda g=g: rs[source, g].astype(jnp.float32) for g in range(GROUPS)], 0, TILE)

    def second_turn(g):
        project_again(g)
        attend(
            g, 1, lambda n: kv[1, g, n],
            lambda n: pick(j0, fr[g, n], sl[g, n]).astype(jnp.bfloat16),
            lambda n: pick(j0, su[g, n], fr[g, n]).astype(jnp.bfloat16),
            rs[source, g].astype(jnp.float32), lambda g, h: None,
        )
        put_out(g)

    for g in range(GROUPS):
        second_turn(g)

    for cp in x_own() + rims:
        cp.wait_send()
    for part in range(4):
        for way in range(2):
            z_copy(part, way, z).wait_send()
    d1_copy(z).wait_send()
    d2_copy(z).wait_send()

    for g, h in each_part:
        stream_copy(g, h).wait_send()

    def drain(s, carry):
        before = plane(-s)
        after = plane(s)
        z_copy(0, 0, before).wait_send()
        x_drain(before)
        d1_copy(before).wait_send()
        d2_copy(before).wait_send()
        for part in (1, 2, 3):
            z_copy(part, 1, after).wait_send()

        @pl.when(s <= 6)
        def _():
            z_copy(0, 1, after).wait_send()
            for part in (1, 2, 3):
                z_copy(part, 0, before).wait_send()

        x_drain(after)
        d1_copy(after).wait_send()
        d2_copy(after).wait_send()
        return carry

    lax.fori_loop(1, 8, drain, 0)
    far = plane(8)
    x_drain(far)
    d1_copy(far).wait_send()
    d2_copy(far).wait_send()


def shards(block_inputs, stale_kv, projection, modulation, pattern, order):
    dma = pltpu.SemaphoreType.DMA
    vmem = pltpu.VMEM
    bf16 = jnp.bfloat16
    out = pl.pallas_call(
        kernel,
        out_shape=pltpu.VMEM((2 * TILE, FEAT), bf16),
        in_specs=[pl.BlockSpec(memory_space=pl.ANY)] * 4
        + [pl.BlockSpec(memory_space=pltpu.VMEM)] * 2,
        out_specs=pl.BlockSpec(memory_space=pltpu.VMEM),
        scratch_shapes=[
            vmem((PLANES, 4, 3, COLS, FEAT), bf16),
            vmem((GROUPS, 3, 4, 4 * COLS, FEAT), bf16),
            vmem((GROUPS, FEAT, 3 * WIDE), bf16),
            vmem((GROUPS, 2 * TILE, WIDE), bf16),
            vmem((GROUPS, 2, 2 * TILE, WIDE), bf16),
            vmem((TILE + RIM, FEAT), bf16),
            vmem((GROUPS, TILE, WIDE), bf16),
            vmem((2, GROUPS, 2, TILE, WIDE), bf16),
            vmem((2, GROUPS, TILE, WIDE), bf16),
            vmem((2, GROUPS, TILE, WIDE), bf16),
            vmem((GROUPS, 2, RIM, WIDE), bf16),
            vmem((GROUPS, 2, RIM, WIDE), bf16),
            vmem((GROUPS, RIM, WIDE), bf16),
            vmem((GROUPS, RIM, WIDE), bf16),
            vmem((GROUPS, 2, RIM, WIDE), bf16),
            vmem((2, WINDOW, HEAD), bf16),
            vmem((8, FEAT), jnp.float32),
            dma((16,)),
            dma((4, 2, PLANES)),
            dma((4, PLANES)),
            dma((2, PLANES)),
            dma((2, PLANES)),
            dma((PLANES,)),
            dma((PLANES,)),
            dma((PLANES,)),
            dma((PLANES,)),
            dma((4,)),
            dma((4,)),
            dma((GROUPS, WIDE // HEAD)),
            dma((GROUPS, WIDE // HEAD)),
        ],
        compiler_params=pltpu.CompilerParams(
            collective_id=0, has_side_effects=True, vmem_limit_bytes=58 * 2**20
        ),
        name="blocks",
    )(
        block_inputs[0],
        stale_kv[0],
        jnp.swapaxes(projection[0], 1, 2),
        jnp.swapaxes(modulation, 0, 1),
        pattern,
        order.reshape(1, 2),
    )
    return out[None]


def solution(mesh):
    placed = (
        P("section", "tile", None),
        P("section", "tile", None),
        P("section", None, None, "tile"),
        P("section", None, None),
        P("tile", None),
        P(),
    )
    return jax.shard_map(
        shards, mesh=mesh, in_specs=placed, out_specs=P("section", "tile", None), check_vma=False
    )
```

```python
import math

import jax
import jax.numpy as jnp
from jax import lax
from jax.experimental import pallas as pl
from jax.experimental.pallas import tpu as pltpu
from jax.sharding import PartitionSpec as P

HEADS = 12
FEAT = 1536
TILE = 192
RIM = 48
PLANES = 16
SECTIONS = 8
TILES = 64
COLS = 24
GROUPS = 4
WIDE = FEAT // GROUPS
HEAD = FEAT // HEADS
WINDOW = 2 * TILE + 2 * RIM
DUP = 1024
EPS = 1e-06
MESH = pl.DeviceIdType.MESH
NT = (((1,), (1,)), ((), ()))
SCALE = math.log2(math.e) / math.sqrt(HEAD)


def kernel(
    x_hbm, stale_hbm, proj_hbm, mod_hbm, pattern_ref, order_ref, out_ref,
    w, dense, turned, xb, st, hidden, q, kv, o, rs, sl, su, xl, xu, fr, marks, mod_ref,
    loc_sem, zs, zr, xs, xr, d1s, d1r, d2s, d2r, rim_s, rim_r, str_s, str_r,
):
    section = lax.axis_index("section")
    tile = lax.axis_index("tile")
    z = tile // 4
    xh = (tile // 2) % 2
    c = tile % 2
    u = xh * 2 + c
    up = (1 - xh) * 2 + c

    def plane(d):
        return (z + d + PLANES) % PLANES

    def at_tile(t):
        return (section, t)

    z_dev = (
        at_tile(((z + 1) % PLANES) * 4 + u),
        at_tile(((z + PLANES - 1) % PLANES) * 4 + u),
    )
    x_dev = at_tile(z * 4 + up)
    sib = at_tile(z * 4 + xh * 2 + (1 - c))
    tile_hi = at_tile((tile + 1) % TILES)
    tile_lo = at_tile((tile + TILES - 1) % TILES)
    sec_hi = ((section + 1) % SECTIONS, tile)
    sec_lo = ((section + SECTIONS - 1) % SECTIONS, tile)

    own_w = pltpu.make_async_copy(proj_hbm, w.at[z, u], loc_sem.at[0])
    own_w.start()
    x_loads = [
        pltpu.make_async_copy(x_hbm.at[:, pl.ds(g * WIDE, WIDE)], xb.at[g], loc_sem.at[1 + g])
        for g in range(GROUPS)
    ]
    st_loads = [
        pltpu.make_async_copy(
            stale_hbm.at[:, pl.ds((k * GROUPS + g) * WIDE, WIDE)], st.at[g, k],
            loc_sem.at[5 + 2 * g + k],
        )
        for g in range(GROUPS)
        for k in range(2)
    ]
    mod_loads = [
        pltpu.make_async_copy(mod_hbm.at[m], mod_ref.at[pl.ds(m, 1)], loc_sem.at[13 + m])
        for m in range(3)
    ]
    for cp in x_loads + st_loads + mod_loads:
        cp.start()

    bar = pltpu.get_barrier_semaphore()
    peers = (z_dev[0], z_dev[1], x_dev, sib, tile_hi, tile_lo, sec_hi, sec_lo)
    for dev in peers:
        pl.semaphore_signal(bar, inc=1, device_id=dev, device_id_type=MESH)
    pl.semaphore_wait(bar, len(peers))

    def remote(src, dst, s, r, dev):
        return pltpu.make_async_remote_copy(
            src_ref=src, dst_ref=dst, send_sem=s, recv_sem=r, device_id=dev, device_id_type=MESH
        )

    def z_copy(part, way, p):
        if part == 0:
            ref = w.at[p, u, pl.ds(0, 2)]
        elif part == 1:
            ref = w.at[p, u, 2]
        elif part == 2:
            ref = w.at[p, up, 2]
        else:
            ref = w.at[p, up, 1, :, pl.ds(0, DUP)]
        return remote(ref, ref, zs.at[part, way, p], zr.at[part, p], z_dev[way])

    def z_wait(part, p):
        z_copy(part, 0, p).wait_recv()

    def x_copies(p):
        refs = (w.at[p, u, 0], w.at[p, u, 1, :, pl.ds(DUP, FEAT - DUP)])
        return [
            remote(ref, ref, xs.at[i, p], xr.at[i, p], x_dev) for i, ref in enumerate(refs)
        ]

    def x_own():
        refs = (w.at[z, u, 0], w.at[z, u, pl.ds(1, 2)])
        return [
            remote(ref, ref, xs.at[i, z], xr.at[i, z], x_dev) for i, ref in enumerate(refs)
        ]

    def x_start(p):
        for cp in x_copies(p):
            cp.start()

    def x_wait(p):
        for cp in x_copies(p):
            cp.wait_recv()

    def x_drain(p):
        for cp in x_copies(p):
            cp.wait_send()

    def d1_copy(p):
        ref = w.at[p, u]
        return remote(ref, ref, d1s.at[p], d1r.at[p], sib)

    def d2_copy(p):
        ref = w.at[p, up]
        return remote(ref, ref, d2s.at[p], d2r.at[p], sib)

    own_w.wait()
    x_own()[1].start()
    x_own()[0].start()
    for part in (0, 1):
        for way in range(2):
            z_copy(part, way, z).start()
    d1_copy(z).start()

    head_rows = pl.ds(0, RIM)
    tail_rows = pl.ds(2 * TILE - RIM, RIM)
    rims = [
        remote(st.at[:, :, head_rows, :], su, rim_s.at[0], rim_r.at[0], tile_lo),
        remote(st.at[:, :, tail_rows, :], sl, rim_s.at[1], rim_r.at[1], tile_hi),
        remote(xb.at[:, head_rows, :], xu, rim_s.at[2], rim_r.at[2], tile_lo),
        remote(xb.at[:, tail_rows, :], xl, rim_s.at[3], rim_r.at[3], tile_hi),
    ]

    parity = section % 2
    first = order_ref[0:1, 0:1]
    second = order_ref[0:1, 1:2]
    j0 = jnp.where(parity == 0, first, second)
    has_lo = jnp.where(tile > 0, 1, 0)
    has_hi = jnp.where(tile < TILES - 1, 1, 0)

    def pick(flag, yes, no):
        on = jnp.broadcast_to(flag, yes.shape) > 0
        return jnp.where(on, yes.astype(jnp.float32), no.astype(jnp.float32))

    def set_marks(turn, j):
        def mark(slot):
            one, two = pattern_ref[0:1, slot : slot + 1], pattern_ref[1:2, slot : slot + 1]
            return one + j * (two - one)

        one, two = mark(1), mark(2)
        spans = (
            (one + j0 * (two - one), TILE),
            (two + j0 * (one - two), TILE),
            (mark(0) * has_lo, RIM),
            (mark(3) * has_hi, RIM),
        )
        start = 0
        for value, width in spans:
            on = jnp.broadcast_to(value, (width, HEAD)) > 0
            marks[turn, pl.ds(start, width), :] = jnp.where(on, 1.0, 0.0).astype(jnp.bfloat16)
            start += width

    def tile_rows(ref, g, j):
        return pick(j, ref[g, TILE : 2 * TILE, :], ref[g, 0:TILE, :])

    def stale_other(g, n):
        one, two = st[g, n, 0:TILE, :], st[g, n, TILE : 2 * TILE, :]
        return pick(j0, one, two).astype(jnp.bfloat16)

    def modulate(parts, start, count):
        total = jnp.zeros((count, 1), jnp.float32)
        for part in parts:
            values = part()
            total = total + jnp.sum(values * values, axis=1, keepdims=True)
        inv = lax.rsqrt(total * (1.0 / FEAT) + EPS)
        for g, part in enumerate(parts):
            cols = pl.ds(g * WIDE, WIDE)
            normed = part() * inv
            hidden[pl.ds(start, count), cols] = (
                (1.0 + mod_ref[1:2, cols]) * normed + mod_ref[0:1, cols]
            ).astype(jnp.bfloat16)

    def head_norm(rows, factor):
        parts = []
        for h in range(WIDE // HEAD):
            one = rows[:, h * HEAD : (h + 1) * HEAD]
            mean = jnp.mean(one * one, axis=1, keepdims=True)
            parts.append(one * (lax.rsqrt(mean + EPS) * factor))
        return jnp.concatenate(parts, axis=1).astype(jnp.bfloat16)

    def turn_weights(g):
        for m in range(3):
            turned[g, :, m * WIDE : (m + 1) * WIDE] = dense[g, m].reshape(WIDE, FEAT).T

    def project_again(g):
        res = jnp.dot(
            hidden[pl.ds(0, TILE), :], turned[g], preferred_element_type=jnp.float32
        )
        q[g] = head_norm(res[:, 0:WIDE], SCALE)
        kv[1, g, 0] = head_norm(res[:, WIDE : 2 * WIDE], 1.0)
        kv[1, g, 1] = res[:, 2 * WIDE : 3 * WIDE].astype(jnp.bfloat16)

    def project(g):
        count = TILE + RIM
        rows = hidden[pl.ds(0, count), :]
        for m in range(3):
            weight = dense[g, m].reshape(WIDE, FEAT)
            res = lax.dot_general(
                rows if m else rows[0:TILE], weight, NT, preferred_element_type=jnp.float32
            )
            low = head_norm(res, 1.0 if m else SCALE) if m < 2 else res.astype(jnp.bfloat16)
            if m == 0:
                q[g] = low
                continue
            kv[0, g, m - 1] = low[0:TILE]
            fr[g, m - 1] = low[TILE:count]

    def columns_of(g):
        start = g * WIDE
        return pl.ds(start if isinstance(g, int) else pl.multiple_of(start, WIDE), WIDE)

    def attend(g, turn, other, low, high, stream, ready):
        def window(k):
            return jnp.concatenate([kv[0, g, k], other(k), low(k), high(k)], axis=0)

        keys = window(0)
        values = window(1)
        queries = q[g]
        mark = marks[turn]
        gate = mod_ref[2:3, columns_of(g)]
        for h in range(WIDE // HEAD):
            cols = slice(h * HEAD, (h + 1) * HEAD)
            scores = lax.dot_general(
                queries[:, cols], keys[:, cols], NT, preferred_element_type=jnp.float32
            )
            unnormed = jnp.exp2(scores).astype(jnp.bfloat16)
            marked = jnp.concatenate([values[:, cols] * mark, mark], axis=1)
            both = jnp.dot(unnormed, marked, preferred_element_type=jnp.float32)
            attended = both[:, :HEAD] / both[:, HEAD:]
            o[turn, g, :, cols] = (stream[:, cols] + gate[:, cols] * attended).astype(jnp.bfloat16)
            ready(g, h)

    def put_out(g):
        early, late = o[0, g], o[1, g]
        cols = pl.ds(g * WIDE, WIDE)
        out_ref[pl.ds(0, TILE), cols] = pick(j0, late, early).astype(jnp.bfloat16)
        out_ref[pl.ds(TILE, TILE), cols] = pick(j0, early, late).astype(jnp.bfloat16)

    def lay_out(p):
        d1_copy(p).wait_recv()
        d2_copy(p).wait_recv()
        for m in range(3):
            parts = [w[p, v, m].astype(jnp.float32) for v in range(4)]
            dense[p // 4, m, p % 4] = jnp.concatenate(parts, axis=0).astype(jnp.bfloat16)

    def stream_copy(g, h):
        cols = pl.ds(h * HEAD, HEAD)
        return remote(
            o.at[0, g, :, cols], rs.at[0, g, :, cols], str_s.at[g, h], str_r.at[g, h], sec_hi
        )

    def send_stream(g, h):
        stream_copy(g, h).start()

    each_part = [(g, h) for g in range(GROUPS) for h in range(WIDE // HEAD)]

    near = jnp.where(z % 4 < 2, GROUPS - 1, 1)

    def group_at(k):
        base = z // 4
        step = jnp.where(k == 0, 0, jnp.where(k == 1, near, jnp.where(k == 2, GROUPS - near, 2)))
        return (base + step) % GROUPS

    def first_turn(k):
        g = group_at(k)
        project(g)
        attend(
            g, 0, lambda n: stale_other(g, n), lambda n: sl[g, n], lambda n: su[g, n],
            tile_rows(xb, g, j0), send_stream,
        )

    x_own()[1].wait_recv()
    for part in (2, 3):
        for way in range(2):
            z_copy(part, way, z).start()
    x_own()[0].wait_recv()
    d2_copy(z).start()

    def prepare():
        for cp in x_loads + st_loads + mod_loads:
            cp.wait()
        for cp in rims:
            cp.start()
        modulate([lambda g=g: tile_rows(xb, g, j0) for g in range(GROUPS)], 0, TILE)
        set_marks(0, j0)
        set_marks(1, 1 - j0)

        @pl.when(section == 0)
        def _():
            for g in range(GROUPS):
                rs[1, g] = tile_rows(xb, g, 1 - j0).astype(jnp.bfloat16)

    def neighbours():
        for cp in rims:
            cp.wait_recv()
        modulate([lambda g=g: pick(j0, xl[g], xu[g]) for g in range(GROUPS)], TILE, RIM)

    def ring_step(s, carry):
        before = plane(-s)
        after = plane(s)

        @pl.when(s <= 8)
        def _():
            z_wait(0, before)

            @pl.when(s <= 7)
            def _():
                z_copy(0, 0, before).start()

            x_start(before)

        @pl.when(s <= 7)
        def _():
            z_wait(0, after)

            @pl.when(s <= 6)
            def _():
                z_copy(0, 1, after).start()

            x_start(after)

        @pl.when(s >= 2)
        def _():
            p = plane(1 - s)
            x_wait(p)
            d2_copy(p).start()

        @pl.when((s >= 2) & (s <= 8))
        def _():
            p = plane(s - 1)
            x_wait(p)
            d2_copy(p).start()

        @pl.when(s <= 7)
        def _():
            for part in (1, 2, 3):
                z_wait(part, before)

                @pl.when(s <= 6)
                def _():
                    z_copy(part, 0, before).start()

            d1_copy(before).start()

        @pl.when(s <= 8)
        def _():
            for part in (1, 2, 3):
                z_wait(part, after)

                @pl.when(s <= 7)
                def _():
                    z_copy(part, 1, after).start()

            d1_copy(after).start()

        @pl.when(s == 1)
        def _():
            prepare()

        @pl.when(s == 3)
        def _():
            neighbours()

        lay_out(plane(1 - s))

        @pl.when((s >= 2) & (s <= 8))
        def _():
            lay_out(plane(s - 1))

        @pl.when((s == 4) | (s == 6) | (s >= 8))
        def _():
            first_turn(jnp.where(s == 9, 3, (s - 4) // 2))

        @pl.when((s == 5) | (s == 7))
        def _():
            turn_weights(group_at((s - 5) // 2))

        return carry

    lax.fori_loop(1, 10, ring_step, 0)

    def last_turned(k, carry):
        turn_weights(group_at(k))
        return carry

    lax.fori_loop(2, GROUPS, last_turned, 0)
    for g, h in each_part:
        stream_copy(g, h).wait_recv()
    source = jnp.where(section == 0, 1, 0)
    modulate([lambda g=g: rs[source, g].astype(jnp.float32) for g in range(GROUPS)], 0, TILE)

    def second_turn(g):
        project_again(g)
        attend(
            g, 1, lambda n: kv[1, g, n],
            lambda n: pick(j0, fr[g, n], sl[g, n]).astype(jnp.bfloat16),
            lambda n: pick(j0, su[g, n], fr[g, n]).astype(jnp.bfloat16),
            rs[source, g].astype(jnp.float32), lambda g, h: None,
        )
        put_out(g)

    for g in range(GROUPS):
        second_turn(g)

    for cp in x_own() + rims:
        cp.wait_send()
    for part in range(4):
        for way in range(2):
            z_copy(part, way, z).wait_send()
    d1_copy(z).wait_send()
    d2_copy(z).wait_send()

    for g, h in each_part:
        stream_copy(g, h).wait_send()

    def drain(s, carry):
        before = plane(-s)
        after = plane(s)
        z_copy(0, 0, before).wait_send()
        x_drain(before)
        d1_copy(before).wait_send()
        d2_copy(before).wait_send()
        for part in (1, 2, 3):
            z_copy(part, 1, after).wait_send()

        @pl.when(s <= 6)
        def _():
            z_copy(0, 1, after).wait_send()
            for part in (1, 2, 3):
                z_copy(part, 0, before).wait_send()

        x_drain(after)
        d1_copy(after).wait_send()
        d2_copy(after).wait_send()
        return carry

    lax.fori_loop(1, 8, drain, 0)
    far = plane(8)
    x_drain(far)
    d1_copy(far).wait_send()
    d2_copy(far).wait_send()


def shards(block_inputs, stale_kv, projection, modulation, pattern, order):
    dma = pltpu.SemaphoreType.DMA
    vmem = pltpu.VMEM
    bf16 = jnp.bfloat16
    out = pl.pallas_call(
        kernel,
        out_shape=pltpu.VMEM((2 * TILE, FEAT), bf16),
        in_specs=[pl.BlockSpec(memory_space=pl.ANY)] * 4
        + [pl.BlockSpec(memory_space=pltpu.VMEM)] * 2,
        out_specs=pl.BlockSpec(memory_space=pltpu.VMEM),
        scratch_shapes=[
            vmem((PLANES, 4, 3, COLS, FEAT), bf16),
            vmem((GROUPS, 3, 4, 4 * COLS, FEAT), bf16),
            vmem((GROUPS, FEAT, 3 * WIDE), bf16),
            vmem((GROUPS, 2 * TILE, WIDE), bf16),
            vmem((GROUPS, 2, 2 * TILE, WIDE), bf16),
            vmem((TILE + RIM, FEAT), bf16),
            vmem((GROUPS, TILE, WIDE), bf16),
            vmem((2, GROUPS, 2, TILE, WIDE), bf16),
            vmem((2, GROUPS, TILE, WIDE), bf16),
            vmem((2, GROUPS, TILE, WIDE), bf16),
            vmem((GROUPS, 2, RIM, WIDE), bf16),
            vmem((GROUPS, 2, RIM, WIDE), bf16),
            vmem((GROUPS, RIM, WIDE), bf16),
            vmem((GROUPS, RIM, WIDE), bf16),
            vmem((GROUPS, 2, RIM, WIDE), bf16),
            vmem((2, WINDOW, HEAD), bf16),
            vmem((8, FEAT), jnp.float32),
            dma((16,)),
            dma((4, 2, PLANES)),
            dma((4, PLANES)),
            dma((2, PLANES)),
            dma((2, PLANES)),
            dma((PLANES,)),
            dma((PLANES,)),
            dma((PLANES,)),
            dma((PLANES,)),
            dma((4,)),
            dma((4,)),
            dma((GROUPS, WIDE // HEAD)),
            dma((GROUPS, WIDE // HEAD)),
        ],
        compiler_params=pltpu.CompilerParams(
            collective_id=0, has_side_effects=True, vmem_limit_bytes=58 * 2**20
        ),
        name="blocks",
    )(
        block_inputs[0],
        stale_kv[0],
        jnp.swapaxes(projection[0], 1, 2),
        jnp.swapaxes(modulation, 0, 1),
        pattern,
        order.reshape(1, 2),
    )
    return out[None]


def solution(mesh):
    placed = (
        P("section", "tile", None),
        P("section", "tile", None),
        P("section", None, None, "tile"),
        P("section", None, None),
        P("tile", None),
        P(),
    )
    return jax.shard_map(
        shards, mesh=mesh, in_specs=placed, out_specs=P("section", "tile", None), check_vma=False
    )
```
